512 devices in a mesh: expert: 64 (over z, y), dp: 8 (over x, core).
Axes of the slice: x: 4, y: 8, z: 8, core: 2. Of those that a mesh axis runs over, the one named last changes fastest.
Arguments:
- attn_win: bfloat16 [64, 1024, 768], P('dp', 'expert'), may hold values from -6 to 6
- shortcut: bfloat16 [64, 1024, 768], P('dp', 'expert'), may hold values from -6 to 6
- d_out: bfloat16 [64, 1024, 768], P('dp', 'expert'), may hold values from -6 to 6
- expert_ids: int32 [8, 64, 128, 2], P('dp', 'expert'), may hold values from 0 to 63, all different within a row; in each aligned block of 128 rows (0 to 127, 128 to 255, ..., all dimensions but the last counted through in order) at most 5 rows name the same one
- gate_probs: float32 [8, 64, 128, 2], P('dp', 'expert'), may hold values from 0.1 to 1
- shift_offsets: int32 [2], replicated, may hold values from 1 to 4, as said below
- w_in: bfloat16 [64, 768, 1536], P('expert', None, 'dp'), may hold values from -0.21875 to 0.21875
- w_out: bfloat16 [64, 1536, 768], P('expert', 'dp'), may hold values from -0.15625 to 0.15625
Outputs:
- block_out: bfloat16 [64, 1024, 768], P('dp', 'expert')
- d_shortcut: bfloat16 [64, 1024, 768], P('dp', 'expert')
- d_attn: bfloat16 [64, 1024, 768], P('dp', 'expert')
- d_gates: float32 [8, 64, 128, 2], P('dp', 'expert')
- grad_in: float32 [64, 768, 1536], P('expert', None, 'dp')
- grad_out: float32 [64, 1536, 768], P('expert', 'dp')
The draws below stay inside these ranges and needn't reach their ends.
Inputs may be any that keep to these rules, and one draw needn't show every extreme that they name: `expert_ids`: in each device's tile no expert is named by more than 5 tokens, a bound that some block reaches. `shift_offsets`: one of the two offsets equals 4.
All inputs are finite; a program needn't handle non-finite values.
Results may differ from the reference program's by a relative error of at most 0.0061.
Values may be sent and summed in bfloat16 or wider, within the bound.
No kernel may reach another device: no remote copies, remote signals or barrier semaphores. Data moves between devices by JAX's collectives and lax.ppermute only.
A program may use at most 128 MiB of HBM per device.

```python
import math
import jax
import jax.numpy as jnp
import numpy as np
from jax import lax

D = 768
FF = 1536
E = 64
TILE_R = 8
TILE_C = 16
SHIFT = 4
CAP = 5
ROWS = 64
COLS = 1024
TOK = 128
N_EXPERT = 64
N_DP = 8


def draw_shift_offsets(key, part):
    key = jax.random.fold_in(key, 7)
    first_key, second_key = jax.random.split(key)
    other = jax.random.randint(first_key, (), 1, SHIFT + 1)
    which = jax.random.randint(second_key, (), 0, 2)
    return jnp.where(jnp.arange(2) == which, SHIFT, other).astype(jnp.int32)


def steps_of(own_key, dims, shards, smallest, largest):
    def one(dim, shards_of):
        steps = jax.random.uniform(jax.random.fold_in(jax.random.fold_in(own_key, 6), dim), (shards_of,), jnp.float32, smallest / len(shards), largest / len(shards))
        return jnp.repeat(jnp.exp(steps), dims[dim] // shards_of).reshape((-1,) + (1,) * (len(dims) - dim - 1))

    loudness = one(*shards[0])
    for cut in shards[1:]:
        loudness = loudness * one(*cut)
    return loudness


def assign_block(stream_key, own, number, rows, count, top, most, lean):
    ranking = jax.random.permutation(stream_key, count)
    packed, usual = load_shares(count, rows * top, most, lean, True), load_shares(count, rows * top, most, lean, False)
    places = jnp.arange(count)

    def named(tallies, offset_by):
        used = int((tallies > 0).sum())
        fixed = max(1, used // 4)
        shifted = fixed + (places - fixed + offset_by * (used - fixed)) % max(1, count - fixed)
        return jnp.zeros((count,), jnp.int32).at[ranking[jnp.where(places < fixed, places, shifted)]].set(jnp.asarray(tallies, jnp.int32))

    tallies = jnp.where(number % 4 == 0, named(packed, number // 4), named(usual, number - number // 4 - 1))
    mixed = jax.random.permutation(jax.random.fold_in(own, 3), count)
    source_of, receiver = mixed[0:count // 2 * 2:2], mixed[1:count // 2 * 2:2]
    room = jnp.minimum(tallies[source_of] - 1, most - tallies[receiver]) // 2
    room = jnp.where((source_of == ranking[0]) | (receiver == ranking[0]) | (tallies[receiver] == 0), 0, jnp.maximum(room, 0))
    shifted = jax.random.randint(jax.random.fold_in(own, 4), (count // 2,), 0, 1 << 20) % (room + 1)
    tallies = tallies.at[source_of].add(-shifted).at[receiver].add(shifted)
    labels = jnp.searchsorted(jnp.cumsum(tallies), jnp.arange(rows * top), side="right").astype(jnp.int32)
    grid = labels.reshape(top, rows).T
    grid = grid[jax.random.permutation(jax.random.fold_in(own, 1), rows)]
    offset_by = jax.random.randint(jax.random.fold_in(own, 2), (rows, 1), 0, top)
    return jnp.take_along_axis(grid, (jnp.arange(top)[None, :] + offset_by) % top, axis=1)


def load_shares(number_of, total, most, skew, full):
    weights = [(1 << 20) // math.isqrt(standing ** skew) + 1 for standing in range(1, number_of + 1)]
    largest = most if full else min(most, max(-(-total // number_of), total * weights[0] // sum(weights)))
    least = 1 if total - largest >= number_of - 1 else 0
    counts, rest = [largest] + [least] * (number_of - 1), total - largest - least * (number_of - 1)
    while rest > 0:
        movable = [i for i in range(1, number_of) if counts[i] < largest] or [i for i in range(1, number_of) if counts[i] < most]
        whole, budget = sum([weights[i] for i in movable]), rest
        for i in movable:
            more = min(most - counts[i], max(1, budget * weights[i] // whole), rest)
            counts[i] = counts[i] + more
            rest = rest - more
    return np.array(counts)


def scatter_about(own_key, shape, spread, reach, shards=(), kind=jnp.bfloat16):
    entries = jax.random.normal(own_key, shape, jnp.float32) * spread
    if len(shards) > 0:
        entries = steps_of(own_key, shape, shards, -0.22, 0.18) * entries
    return jnp.clip(entries, min=-reach, max=reach).astype(kind)


def setup_inputs(seed: int = 0) -> dict:
    splits = jax.random.split(jax.random.key(seed), 9)
    attn_win = scatter_about(splits[0], (ROWS, COLS, D), 1.0, 6.0, ((0, 8), (1, 64)))
    shortcut = scatter_about(splits[1], (ROWS, COLS, D), 1.0, 6.0, ((0, 8), (1, 64)))
    d_out = scatter_about(splits[2], (ROWS, COLS, D), 1.0, 6.0, ((0, 8), (1, 64)))
    expert_ids_keys = jax.random.split(jax.random.fold_in(splits[3], 1), N_DP * N_EXPERT * TOK // TOK)
    expert_ids_turns = jax.random.permutation(jax.random.fold_in(splits[3], 3), N_DP * N_EXPERT * TOK // TOK)
    expert_ids = jax.vmap(lambda own, number: assign_block(jax.random.fold_in(splits[3], 2), own, number, TOK, E, 2, CAP, 2))(expert_ids_keys, expert_ids_turns).reshape((N_DP, N_EXPERT, TOK, 2))
    gate_probs = jnp.clip(0.1 + 0.9 * jax.random.uniform(splits[4], (N_DP, N_EXPERT, TOK, 2), jnp.float32) ** steps_of(splits[4], (N_DP, N_EXPERT, TOK, 2), ((0, 8), (1, 64)), -0.2, 0.2), 0.1, 1.0)
    shift_offsets = draw_shift_offsets(jax.random.fold_in(splits[8], 71), 0)
    w_in = scatter_about(splits[6], (E, D, FF), D ** -0.5, 0.21875, ((0, 64), (2, 8)))
    w_out = scatter_about(splits[7], (E, FF, D), FF ** -0.5, 0.15625, ((0, 64), (1, 8)))
    return dict(attn_win=attn_win, shortcut=shortcut, d_out=d_out, expert_ids=expert_ids, gate_probs=gate_probs, shift_offsets=shift_offsets, w_in=w_in, w_out=w_out)


def slope_of(hidden):
    cdf = 0.5 * (1.0 + lax.erf(hidden * 0.7071067811865476))
    pdf = jnp.exp(-0.5 * hidden * hidden) * 0.3989422804014327
    return cdf + hidden * pdf

def split_into_tiles(field):
    shaped = field.reshape(N_DP, TILE_R, N_EXPERT, TILE_C, -1)
    return shaped.transpose(0, 2, 1, 3, 4).reshape(N_DP, N_EXPERT, TILE_R * TILE_C, -1)

def to_grid(tiles):
    shaped = tiles.reshape(N_DP, N_EXPERT, TILE_R, TILE_C, -1)
    return shaped.transpose(0, 2, 1, 3, 4).reshape(N_DP * TILE_R, N_EXPERT * TILE_C, -1)

def fill_slots(slot_tile, values):
    empty = jnp.zeros((E * CAP, values.shape[-1]), jnp.bfloat16)
    return empty.at[slot_tile.reshape(-1)].set(values.reshape(-1, values.shape[-1]))

def expert_rows(buffers):
    shaped = buffers.reshape(N_DP, N_EXPERT, E, CAP, D)
    return shaped.transpose(2, 0, 1, 3, 4).reshape(E, N_DP * N_EXPERT * CAP, D)

def slot_rows(rows):
    shaped = rows.reshape(E, N_DP, N_EXPERT, CAP, D)
    return shaped.transpose(1, 2, 0, 3, 4).reshape(N_DP, N_EXPERT, E * CAP, D)

def one_expert(operands):
    inputs, cotangent, first, second = operands
    hidden = jnp.dot(inputs, first, preferred_element_type=jnp.float32)
    act = jax.nn.gelu(hidden, approximate=False).astype(jnp.bfloat16)
    result = jnp.dot(act, second, preferred_element_type=jnp.float32).astype(jnp.bfloat16)
    dact = jnp.dot(cotangent, second.T, preferred_element_type=jnp.float32)
    dhid = (dact * slope_of(hidden)).astype(jnp.bfloat16)
    dinp = jnp.dot(dhid, first.T, preferred_element_type=jnp.float32).astype(jnp.bfloat16)
    grad_first = jnp.dot(inputs.T, dhid, preferred_element_type=jnp.float32)
    grad_second = jnp.dot(act.T, cotangent, preferred_element_type=jnp.float32)
    return (result, dinp, grad_first, grad_second)

def reference(attn_win, shortcut, d_out, expert_ids, gate_probs, shift_offsets, w_in, w_out):
    row_off = shift_offsets[0]
    col_off = shift_offsets[1]
    rolled = jnp.roll(jnp.roll(attn_win.astype(jnp.float32), row_off, axis=0), col_off, axis=1)
    x = shortcut.astype(jnp.float32) + rolled
    feature_average = lax.optimization_barrier(jnp.mean(x, axis=-1, keepdims=True))
    centered_input = x - feature_average
    inverse_deviation = lax.rsqrt(lax.optimization_barrier(jnp.mean(centered_input * centered_input, axis=-1, keepdims=True)) + 1e-05)
    standardized_input = centered_input * inverse_deviation
    update_tiles = split_into_tiles(standardized_input.astype(jnp.bfloat16))
    onehot = (expert_ids[..., None] == jnp.arange(E, dtype=jnp.int32)).astype(jnp.int32)
    flat = onehot.reshape(N_DP, N_EXPERT, 2 * TOK, E)
    before = jnp.cumsum(flat, axis=2) - flat
    pos = lax.optimization_barrier(jnp.sum(before * flat, axis=-1)).reshape(N_DP, N_EXPERT, TOK, 2)
    slot = (expert_ids * CAP + pos).astype(jnp.int32)
    u_pairs = jnp.broadcast_to(update_tiles[:, :, :, None, :], (N_DP, N_EXPERT, TOK, 2, D))
    u_buf = jax.vmap(jax.vmap(fill_slots))(slot, u_pairs)
    dout_tiles = split_into_tiles(d_out).astype(jnp.float32)
    weighted = (gate_probs[..., None] * dout_tiles[:, :, :, None, :]).astype(jnp.bfloat16)
    g_buf = jax.vmap(jax.vmap(fill_slots))(slot, weighted)
    results, dinps, grad_in, grad_out = lax.map(one_expert, (expert_rows(u_buf), expert_rows(g_buf), w_in, w_out))
    y_buf = slot_rows(results)
    q_buf = slot_rows(dinps)
    take = jax.vmap(jax.vmap(lambda buf, idx: jnp.take(buf, idx, axis=0)))
    y_tok = take(y_buf, slot).astype(jnp.float32)
    q_tok = take(q_buf, slot).astype(jnp.float32)
    moe = gate_probs[..., 0:1] * y_tok[:, :, :, 0, :] + gate_probs[..., 1:2] * y_tok[:, :, :, 1, :]
    block_out = (x + to_grid(moe)).astype(jnp.bfloat16)
    d_gates = lax.optimization_barrier(jnp.sum(dout_tiles[:, :, :, None, :] * y_tok, axis=-1))
    upstream_gradient = to_grid(q_tok[:, :, :, 0, :] + q_tok[:, :, :, 1, :])
    layernorm_input_gradient = inverse_deviation * (upstream_gradient - lax.optimization_barrier(jnp.mean(upstream_gradient, axis=-1, keepdims=True)) - standardized_input * lax.optimization_barrier(jnp.mean(upstream_gradient * standardized_input, axis=-1, keepdims=True)))
    dx = d_out.astype(jnp.float32) + layernorm_input_gradient
    d_shortcut = dx.astype(jnp.bfloat16)
    d_attn = jnp.roll(jnp.roll(d_shortcut, -row_off, axis=0), -col_off, axis=1)
    return (block_out, d_shortcut, d_attn, d_gates, grad_in, grad_out)
```

```python
import functools

import jax
import jax.numpy as jnp
from jax import lax
from jax.experimental import pallas as pl
from jax.experimental.pallas import tpu as pltpu
from jax.sharding import PartitionSpec as P

CAP = 5
WIRE_ROWS = 8
WIDE = 512
EPS = 1e-05
VMEM = pl.BlockSpec(memory_space=pltpu.VMEM)
SMEM = pl.BlockSpec(memory_space=pltpu.SMEM)


def iota(shape, dim):
    return lax.broadcasted_iota(jnp.int32, shape, dim)


def ones_where(mask):
    return jnp.where(mask, 1.0, 0.0).astype(jnp.bfloat16)


def dot(a, b):
    return jnp.dot(a, b, preferred_element_type=jnp.float32)


def dot_t(a, b):
    return lax.dot_general(a, b, (((1,), (1,)), ((), ())), preferred_element_type=jnp.float32)


def t_dot(a, b):
    return lax.dot_general(a, b, (((0,), (0,)), ((), ())), preferred_element_type=jnp.float32)


def call(body, outs, *args, flops=0, traffic=0, specs=None, **kw):
    return pl.pallas_call(
        body,
        out_shape=outs,
        in_specs=[VMEM] * len(args) if specs is None else specs,
        out_specs=jax.tree.map(lambda _: VMEM, outs),
        compiler_params=pltpu.CompilerParams(vmem_limit_bytes=32 * 1024 * 1024),
        cost_estimate=pl.CostEstimate(flops=flops, bytes_accessed=traffic, transcendentals=0),
        **kw,
    )(*args)


def wire_masks(row, n):
    at = iota((row.shape[0], n), 1)
    pos = row & 7
    tail = row - pos + CAP + (pos >> 1)
    odd = (pos & 1) == 1
    left = jnp.where(odd, -1, tail)
    right = jnp.where(odd, tail, -1)
    return ones_where(at == row), ones_where(at == left), ones_where(at == right)


def from_wire(masks, wire):
    head, left, right = masks
    half = WIDE // 2
    return (
        dot(head, wire),
        dot(left, wire[:, :half]) + dot(right, wire[:, half:]),
    )


def to_wire(masks, rows, turned):
    head, left, right = masks
    f = t_dot if turned else dot
    tail = rows[:, WIDE:]
    return f(head, rows[:, :WIDE]) + jnp.concatenate([f(left, tail), f(right, tail)], axis=1)


def dispatch_g(ids_ref, gates_ref, dout_ref, sent_ref, row_ref):
    tokens = ids_ref.shape[0]
    n = sent_ref.shape[0]
    experts = n // WIRE_ROWS
    ids = ids_ref[...]
    lane = iota((tokens, experts), 1)
    first = jnp.where(ids[:, 0:1] == lane, 1.0, 0.0)
    second = jnp.where(ids[:, 1:2] == lane, 1.0, 0.0)
    lower = ones_where(iota((tokens, tokens), 0) > iota((tokens, tokens), 1))
    before = dot(lower, (first + second).astype(jnp.bfloat16))
    pos0 = jnp.sum(before * first, axis=1, keepdims=True).astype(jnp.int32)
    pos1 = jnp.sum(before * second, axis=1, keepdims=True).astype(jnp.int32)
    row0 = ids[:, 0:1] * WIRE_ROWS + pos0
    row1 = ids[:, 1:2] * WIRE_ROWS + pos1
    row_ref[:, 0:1] = row0
    row_ref[:, 1:2] = row1
    dout = dout_ref[...].astype(jnp.float32)
    gates = gates_ref[...]
    g = jnp.concatenate(
        [(gates[:, 0:1] * dout).astype(jnp.bfloat16), (gates[:, 1:2] * dout).astype(jnp.bfloat16)], axis=0
    )
    row = jnp.concatenate([row0, row1], axis=0)
    sent_ref[...] = to_wire(wire_masks(row, n), g, True).astype(jnp.bfloat16)


def normalize(x):
    m = jnp.mean(x, axis=-1, keepdims=True)
    c = x - m
    r = lax.rsqrt(jnp.mean(c * c, axis=-1, keepdims=True) + EPS)
    return c * r, r


def shifted(i, j, tr, tc, own, row_edge, col_edge, corner):
    i_in = (i >= 0) & (i < tr)
    j_in = (j >= 0) & (j < tc)
    ei = jnp.where(i < 0, i + 4, i - tr)
    ej = jnp.where(j < 0, j + 4, j - tc)

    def pick(mask, index, src):
        index = jnp.where(mask, index, -1)
        return dot(ones_where(index == iota((index.shape[0], src.shape[0]), 1)), src)

    return (
        pick(i_in & j_in, i * tc + j, own)
        + pick((~i_in) & j_in, ei * tc + j, row_edge)
        + pick(i_in & (~j_in), i * 4 + ej, col_edge)
        + pick((~i_in) & (~j_in), ei * 4 + ej, corner)
    )


def dispatch_u(tr, tc, off_ref, row_ref, short_ref, attn_ref, up_ref, left_ref, corner_ref, sent_ref, x_ref):
    tokens = short_ref.shape[0]
    t = iota((tokens, 1), 0)
    i = t // tc - off_ref[0]
    j = t % tc - off_ref[1]
    rolled = shifted(i, j, tr, tc, attn_ref[...], up_ref[...], left_ref[...], corner_ref[...])
    x = short_ref[...].astype(jnp.float32) + rolled
    x_ref[...] = x
    xhat, _ = normalize(x)
    u = xhat.astype(jnp.bfloat16)
    u = jnp.concatenate([u, u], axis=0)
    row = jnp.concatenate([row_ref[:, 0:1], row_ref[:, 1:2]], axis=0)
    sent_ref[...] = to_wire(wire_masks(row, sent_ref.shape[0]), u, True).astype(jnp.bfloat16)


def experts_body(rg_ref, ru_ref, w_ref, q_ref, y_ref, grad_ref, u_s, g_s, q_s, y_s):
    step = pl.program_id(0)
    n = rg_ref.shape[0]
    peers = n // WIRE_ROWS
    slots = peers * CAP

    @pl.when(step == 0)
    def _():
        s = iota((slots, 1), 0)
        masks = wire_masks((s % peers) * WIRE_ROWS + s // peers, n)
        for src, dst in ((ru_ref, u_s), (rg_ref, g_s)):
            head, tail = from_wire(masks, src[...])
            dst[:, :WIDE] = head.astype(jnp.bfloat16)
            dst[:, WIDE:] = tail.astype(jnp.bfloat16)

    u = u_s[...]
    g = g_s[...]
    block, _, part, width = w_ref.shape
    w1 = w_ref[:, 0].reshape(block * part, width)
    w2 = w_ref[:, 1].reshape(block * part, width)
    h = dot_t(u, w1)
    da = dot_t(g, w2)
    cdf = 0.5 * (1.0 + lax.erf(h * 0.7071067811865476))
    pdf = jnp.exp(-0.5 * h * h) * 0.3989422804014327
    a = (h * cdf).astype(jnp.bfloat16)
    p = (da * (cdf + h * pdf)).astype(jnp.bfloat16)
    q = dot(p, w1)
    y = dot(a, w2)
    grad_ref[:, 0] = t_dot(p, u).astype(jnp.bfloat16).reshape(block, part, width)
    grad_ref[:, 1] = t_dot(a, g).astype(jnp.bfloat16).reshape(block, part, width)

    @pl.when(step == 0)
    def _():
        q_s[...] = q
        y_s[...] = y

    @pl.when(step > 0)
    def _():
        q_s[...] += q
        y_s[...] += y

    @pl.when(step == pl.num_programs(0) - 1)
    def _():
        s = iota((slots, 1), 0)
        masks = wire_masks((s % peers) * WIRE_ROWS + s // peers, n)
        q_ref[...] = to_wire(masks, q_s[...].astype(jnp.bfloat16), True).astype(jnp.bfloat16)
        y_ref[...] = to_wire(masks, y_s[...].astype(jnp.bfloat16), True).astype(jnp.bfloat16)


def experts(rg, ru, w):
    n = rg.shape[0]
    parts, _, part, width = w.shape
    slots = n // WIRE_ROWS * CAP
    block = 2
    hidden = parts * part
    whole = pl.BlockSpec((n, WIDE), lambda i: (0, 0))
    piece = pl.BlockSpec((block, 2, part, width), lambda i: (i, 0, 0, 0))
    wire = jax.ShapeDtypeStruct((n, WIDE), jnp.bfloat16)
    return pl.pallas_call(
        experts_body,
        grid=(parts // block,),
        out_shape=(wire, wire, jax.ShapeDtypeStruct(w.shape, jnp.bfloat16)),
        in_specs=[whole, whole, piece],
        out_specs=(whole, whole, piece),
        scratch_shapes=[
            pltpu.VMEM((slots, width), jnp.bfloat16),
            pltpu.VMEM((slots, width), jnp.bfloat16),
            pltpu.VMEM((slots, width), jnp.float32),
            pltpu.VMEM((slots, width), jnp.float32),
        ],
        compiler_params=pltpu.CompilerParams(
            dimension_semantics=("arbitrary",), vmem_limit_bytes=48 * 1024 * 1024
        ),
        cost_estimate=pl.CostEstimate(
            flops=12 * slots * hidden * width,
            bytes_accessed=8 * hidden * width,
            transcendentals=2 * slots * hidden,
        ),
    )(rg, ru, w)


def combine_q(tr, tc, rq_ref, row_ref, x_ref, dout_ref, ds_ref, up_ref, left_ref, corner_ref):
    wire = rq_ref[...]
    masks = [wire_masks(row_ref[:, k : k + 1], wire.shape[0]) for k in range(2)]
    both = tuple(a + b for a, b in zip(*masks))
    du = jnp.concatenate(from_wire(both, wire), axis=1)
    xhat, r = normalize(x_ref[...])
    dx = r * (
        du
        - jnp.mean(du, axis=-1, keepdims=True)
        - xhat * jnp.mean(du * xhat, axis=-1, keepdims=True)
    )
    ds = (dout_ref[...].astype(jnp.float32) + dx).astype(jnp.bfloat16)
    ds_ref[...] = ds
    up_ref[...] = ds[: 4 * tc]
    n = 4 * tr
    s = iota((n, 1), 0)
    edge = dot(ones_where((s // 4) * tc + s % 4 == iota((n, ds.shape[0]), 1)), ds).astype(jnp.bfloat16)
    left_ref[...] = edge
    corner_ref[...] = edge[:16]


def roll_back(tr, tc, off_ref, ds_ref, down_ref, right_ref, corner_ref, out_ref):
    t = iota((ds_ref.shape[0], 1), 0)
    i = t // tc + off_ref[0]
    j = t % tc + off_ref[1]
    out_ref[...] = shifted(
        i, j, tr, tc, ds_ref[...], down_ref[...], right_ref[...], corner_ref[...]
    ).astype(jnp.bfloat16)


def combine_y(ry_ref, row_ref, gates_ref, x_ref, dout_ref, out_ref, dg_ref):
    wire = ry_ref[...]
    dout = dout_ref[...].astype(jnp.float32)
    gates = gates_ref[...]
    total = x_ref[...]
    for k in range(2):
        y = jnp.concatenate(from_wire(wire_masks(row_ref[:, k : k + 1], wire.shape[0]), wire), axis=1)
        total = total + gates[:, k : k + 1] * y
        dg_ref[:, k : k + 1] = jnp.sum(dout * y, axis=-1, keepdims=True)
    out_ref[...] = total.astype(jnp.bfloat16)


def exchange(wire, n):
    wire = wire.reshape(n, WIRE_ROWS, WIDE)
    out = lax.all_to_all(wire, "expert", split_axis=0, concat_axis=0, tiled=True)
    return out.reshape(n * WIRE_ROWS, WIDE)


def edges(row_edge, col_edge, corner, step):
    n_dp, n_ex = lax.axis_size("dp"), lax.axis_size("expert")
    by_dp = [(i, (i + step) % n_dp) for i in range(n_dp)]
    by_ex = [(i, (i + step) % n_ex) for i in range(n_ex)]
    by_both = [
        (q * n_dp + p, (q + step) % n_ex * n_dp + (p + step) % n_dp)
        for q in range(n_ex)
        for p in range(n_dp)
    ]
    return (
        lax.ppermute(row_edge, "dp", by_dp),
        lax.ppermute(col_edge, "expert", by_ex),
        lax.ppermute(corner, ("expert", "dp"), by_both),
    )


def per_device(attn_win, shortcut, d_out, expert_ids, gate_probs, shift_offsets, w_in, w_out):
    tr, tc, width = attn_win.shape
    tokens = tr * tc
    n_ex = lax.axis_size("expert")
    n = n_ex * WIRE_ROWS
    bf16 = functools.partial(jax.ShapeDtypeStruct, dtype=jnp.bfloat16)
    f32 = functools.partial(jax.ShapeDtypeStruct, dtype=jnp.float32)
    ids = expert_ids.reshape(tokens, 2)
    gates = gate_probs.reshape(tokens, 2)
    dout = d_out.reshape(tokens, width)
    attn = attn_win.reshape(tokens, width)
    short = shortcut.reshape(tokens, width)

    w_own = jnp.concatenate([w_in.transpose(0, 2, 1), w_out], axis=0)[None]
    w_all = lax.all_gather(w_own, "dp", axis=0, tiled=True)

    col_edge = attn_win[:, tc - 4 :]
    up, left, corner = edges(
        attn_win[tr - 4 :].reshape(4 * tc, width),
        col_edge.reshape(tr * 4, width),
        col_edge[tr - 4 :].reshape(16, width),
        1,
    )
    sent_g, row = call(
        dispatch_g,
        (bf16((n, WIDE)), jax.ShapeDtypeStruct((tokens, 2), jnp.int32)),
        ids, gates, dout,
        flops=4 * 256 * n * WIDE, traffic=1 << 20,
    )
    rg = exchange(sent_g, n_ex)
    sent_u, x = call(
        functools.partial(dispatch_u, tr, tc),
        (bf16((n, WIDE)), f32((tokens, width))),
        shift_offsets, row, short, attn, up, left, corner,
        specs=[SMEM] + [VMEM] * 6,
        flops=4 * 256 * n * WIDE, traffic=1 << 21,
    )
    ru = exchange(sent_u, n_ex)
    q_wire, y_wire, grads = experts(rg, ru, w_all)
    rq = exchange(q_wire, n_ex)
    ry = exchange(y_wire, n_ex)
    grad = lax.psum_scatter(grads, "dp", scatter_dimension=0, tiled=True).astype(jnp.float32)
    grad_in = grad[:, 0].transpose(0, 2, 1)
    grad_out = grad[:, 1]
    ds, up_b, left_b, corner_b = call(
        functools.partial(combine_q, tr, tc),
        (bf16((tokens, width)), bf16((4 * tc, width)), bf16((4 * tr, width)), bf16((16, width))),
        rq, row, x, dout,
        flops=4 * tokens * n * WIDE, traffic=1 << 21,
    )
    down, right, corner_r = edges(up_b, left_b, corner_b, -1)
    block_out, d_gates = call(
        combine_y,
        (bf16((tokens, width)), f32((tokens, 2))),
        ry, row, gates, x, dout,
        flops=8 * tokens * n * WIDE, traffic=1 << 21,
    )
    d_attn = call(
        functools.partial(roll_back, tr, tc),
        bf16((tokens, width)),
        shift_offsets, ds, down, right, corner_r,
        specs=[SMEM] + [VMEM] * 4,
        flops=2 * tokens * 256 * width, traffic=1 << 19,
    )
    tile = (tr, tc, width)
    return (
        block_out.reshape(tile),
        ds.reshape(tile),
        d_attn.reshape(tile),
        d_gates.reshape(1, 1, tokens, 2),
        grad_in,
        grad_out,
    )


def solution(mesh):
    tile = P("dp", "expert", None)
    pairs = P("dp", "expert", None, None)
    first, second = P("expert", None, "dp"), P("expert", "dp", None)
    return jax.shard_map(
        per_device,
        mesh=mesh,
        in_specs=(tile, tile, tile, pairs, pairs, P(), first, second),
        out_specs=(tile, tile, tile, pairs, first, second),
        check_vma=False,
    )
```

```python
import functools

import jax
import jax.numpy as jnp
from jax import lax
from jax.experimental import pallas as pl
from jax.experimental.pallas import tpu as pltpu
from jax.sharding import PartitionSpec as P

CAP = 5
WIRE_ROWS = 8
WIDE = 512
EPS = 1e-05
VMEM = pl.BlockSpec(memory_space=pltpu.VMEM)
ANY = pl.BlockSpec(memory_space=pl.ANY)
SMEM = pl.BlockSpec(memory_space=pltpu.SMEM)


def iota(shape, dim):
    return lax.broadcasted_iota(jnp.int32, shape, dim)


def ones_where(mask):
    return jnp.where(mask, 1.0, 0.0).astype(jnp.bfloat16)


def dot(a, b):
    return jnp.dot(a, b, preferred_element_type=jnp.float32)


def dot_t(a, b):
    return lax.dot_general(a, b, (((1,), (1,)), ((), ())), preferred_element_type=jnp.float32)


def t_dot(a, b):
    return lax.dot_general(a, b, (((0,), (0,)), ((), ())), preferred_element_type=jnp.float32)


def call(body, outs, *args, flops=0, traffic=0, specs=None, **kw):
    return pl.pallas_call(
        body,
        out_shape=outs,
        in_specs=[VMEM] * len(args) if specs is None else specs,
        out_specs=jax.tree.map(lambda _: VMEM, outs),
        compiler_params=pltpu.CompilerParams(vmem_limit_bytes=32 * 1024 * 1024),
        cost_estimate=pl.CostEstimate(flops=flops, bytes_accessed=traffic, transcendentals=0),
        **kw,
    )(*args)


def wire_masks(row, shape, dim):
    at = iota(shape, dim)
    pos = row & 7
    tail = row - pos + CAP + (pos >> 1)
    odd = (pos & 1) == 1
    left = jnp.where(odd, -1, tail)
    right = jnp.where(odd, tail, -1)
    return ones_where(at == row), ones_where(at == left), ones_where(at == right)


def from_wire(masks, wire):
    head, left, right = masks
    half = WIDE // 2
    return (
        dot(head, wire),
        dot(left, wire[:, :half]) + dot(right, wire[:, half:]),
    )


def to_wire(masks, rows, turned):
    head, left, right = masks
    f = t_dot if turned else dot
    tail = rows[:, WIDE:]
    return f(head, rows[:, :WIDE]) + jnp.concatenate([f(left, tail), f(right, tail)], axis=1)


def prepare(attn_hbm, w1_hbm, w2_hbm, up_ref, left_ref, corner_ref, w_hbm, attn_s, sems):
    copies = [
        pltpu.make_async_copy(src, dst, sems.at[i])
        for i, (src, dst) in enumerate(
            ((attn_hbm, attn_s), (w1_hbm, w_hbm.at[:, 0]), (w2_hbm, w_hbm.at[:, 1]))
        )
    ]
    for copy in copies:
        copy.start()
    tr, tc, width = attn_s.shape
    tokens = tr * tc
    n = 4 * tr
    s = iota((n, 1), 0)
    edge = ones_where((s // 4) * tc + tc - 4 + s % 4 == iota((n, tokens), 1))
    copies[0].wait()
    attn = attn_s[...].reshape(tokens, width)
    up_ref[...] = attn[tokens - 4 * tc :]
    left = dot(edge, attn).astype(jnp.bfloat16)
    left_ref[...] = left
    corner_ref[...] = left[n - 16 :]
    copies[1].wait()
    copies[2].wait()


def dispatch_g(tr, tc, off_ref, ids_ref, gates_ref, dout_ref, attn_ref, short_ref, sent_ref, mask_ref, meta_ref, x_ref, sel_ref):
    tokens = dout_ref.shape[0]
    t = iota((tokens, 1), 0)
    inside, halo = places(t // tc - off_ref[0], t % tc - off_ref[1], tr, tc)
    sel_ref[...] = halo
    x_ref[...] = short_ref[...].astype(jnp.float32) + dot(inside, attn_ref[...])
    n = sent_ref.shape[0]
    experts = n // WIRE_ROWS
    ids = ids_ref[...]
    rank = iota((experts, tokens), 0)
    first = jnp.where(ids[0:1] == rank, 1.0, 0.0)
    second = jnp.where(ids[1:2] == rank, 1.0, 0.0)
    earlier = ones_where(iota((tokens, tokens), 0) < iota((tokens, tokens), 1))
    before = dot((first + second).astype(jnp.bfloat16), earlier)
    row0 = ids[0:1] * WIRE_ROWS + jnp.sum(before * first, axis=0, keepdims=True).astype(jnp.int32)
    row1 = ids[1:2] * WIRE_ROWS + jnp.sum(before * second, axis=0, keepdims=True).astype(jnp.int32)
    at = iota((tokens, tokens), 0)
    table = jnp.where(at == 0, gates_ref[0:1], 0.0)
    table = jnp.where(at == 1, gates_ref[1:2], table)
    table = jnp.where(at == 2, row0.astype(jnp.float32), table)
    table = jnp.where(at == 3, row1.astype(jnp.float32), table)
    meta = table.T
    meta_ref[...] = meta
    dout = dout_ref[...].astype(jnp.float32)
    sent = 0.0
    both = None
    for k, row in enumerate((row0, row1)):
        masks = wire_masks(row, (n, tokens), 0)
        sent = sent + to_wire(masks, (meta[:, k : k + 1] * dout).astype(jnp.bfloat16), False)
        both = masks if both is None else tuple(a + b for a, b in zip(both, masks))
    for m in range(3):
        mask_ref[m] = both[m]
    sent_ref[...] = sent.astype(jnp.bfloat16)


def normalize(x):
    m = jnp.mean(x, axis=-1, keepdims=True)
    c = x - m
    r = lax.rsqrt(jnp.mean(c * c, axis=-1, keepdims=True) + EPS)
    return c * r, r


def places(i, j, tr, tc):
    tokens = i.shape[0]
    i_in = (i >= 0) & (i < tr)
    j_in = (j >= 0) & (j < tc)
    ei = jnp.where(i < 0, i + 4, i - tr)
    ej = jnp.where(j < 0, j + 4, j - tc)
    own = jnp.where(i_in & j_in, i * tc + j, -1)
    edge = jnp.where(
        i_in,
        jnp.where(j_in, -1, 4 * tc + i * 4 + ej),
        jnp.where(j_in, ei * tc + j, 4 * tc + 4 * tr + ei * 4 + ej),
    )
    count = 4 * tc + 4 * tr + 16
    return (
        ones_where(own == iota((tokens, tokens), 1)),
        ones_where(edge == iota((tokens, count), 1)),
    )


def dispatch_u(g_ref, mask_ref, x0_ref, sel_ref, up_ref, left_ref, corner_ref, sent_ref, x_ref):
    edge = jnp.concatenate([up_ref[...], left_ref[...], corner_ref[...]], axis=0)
    x = x0_ref[...] + dot(sel_ref[...], edge)
    x_ref[...] = x
    xhat, _ = normalize(x)
    masks = tuple(mask_ref[m] for m in range(3))
    sent_ref[:, :WIDE] = g_ref[...]
    sent_ref[:, WIDE:] = to_wire(masks, xhat.astype(jnp.bfloat16), False).astype(jnp.bfloat16)


def experts_body(wire_ref, w_ref, out_ref, grad_ref, u_s, g_s, q_s, y_s):
    step = pl.program_id(0)
    n = wire_ref.shape[0]
    peers = n // WIRE_ROWS
    slots = peers * CAP

    @pl.when(step == 0)
    def _():
        s = iota((slots, 1), 0)
        masks = wire_masks((s % peers) * WIRE_ROWS + s // peers, (slots, n), 1)
        for at, dst in ((0, g_s), (WIDE, u_s)):
            head, tail = from_wire(masks, wire_ref[:, at : at + WIDE])
            dst[:, :WIDE] = head.astype(jnp.bfloat16)
            dst[:, WIDE:] = tail.astype(jnp.bfloat16)

    u = u_s[...]
    g = g_s[...]
    block, _, part, width = w_ref.shape
    w1 = w_ref[:, 0].reshape(block * part, width)
    w2 = w_ref[:, 1].reshape(block * part, width)
    h = dot_t(u, w1)
    da = dot_t(g, w2)
    cdf = 0.5 * (1.0 + lax.erf(h * 0.7071067811865476))
    pdf = jnp.exp(-0.5 * h * h) * 0.3989422804014327
    a = (h * cdf).astype(jnp.bfloat16)
    p = (da * (cdf + h * pdf)).astype(jnp.bfloat16)
    q = dot(p, w1)
    y = dot(a, w2)
    grad_ref[:, 0] = t_dot(p, u).astype(jnp.bfloat16).reshape(block, part, width)
    grad_ref[:, 1] = t_dot(a, g).astype(jnp.bfloat16).reshape(block, part, width)

    @pl.when(step == 0)
    def _():
        q_s[...] = q
        y_s[...] = y

    @pl.when(step > 0)
    def _():
        q_s[...] += q
        y_s[...] += y

    @pl.when(step == pl.num_programs(0) - 1)
    def _():
        s = iota((slots, 1), 0)
        masks = wire_masks((s % peers) * WIRE_ROWS + s // peers, (slots, n), 1)
        out_ref[:, :WIDE] = to_wire(masks, q_s[...].astype(jnp.bfloat16), True).astype(jnp.bfloat16)
        out_ref[:, WIDE:] = to_wire(masks, y_s[...].astype(jnp.bfloat16), True).astype(jnp.bfloat16)


def experts(wire, w):
    n = wire.shape[0]
    parts, _, part, width = w.shape
    slots = n // WIRE_ROWS * CAP
    block = 2
    hidden = parts * part
    whole = pl.BlockSpec((n, 2 * WIDE), lambda i: (0, 0))
    piece = pl.BlockSpec((block, 2, part, width), lambda i: (i, 0, 0, 0))
    return pl.pallas_call(
        experts_body,
        grid=(parts // block,),
        out_shape=(
            jax.ShapeDtypeStruct((n, 2 * WIDE), jnp.bfloat16),
            jax.ShapeDtypeStruct(w.shape, jnp.bfloat16),
        ),
        in_specs=[whole, piece],
        out_specs=(whole, piece),
        scratch_shapes=[
            pltpu.VMEM((slots, width), jnp.bfloat16),
            pltpu.VMEM((slots, width), jnp.bfloat16),
            pltpu.VMEM((slots, width), jnp.float32),
            pltpu.VMEM((slots, width), jnp.float32),
        ],
        compiler_params=pltpu.CompilerParams(
            dimension_semantics=("arbitrary",), vmem_limit_bytes=48 * 1024 * 1024
        ),
        cost_estimate=pl.CostEstimate(
            flops=12 * slots * hidden * width,
            bytes_accessed=8 * hidden * width,
            transcendentals=2 * slots * hidden,
        ),
    )(wire, w)


def combine_q(tr, tc, wire_ref, meta_ref, x_ref, dout_ref, ds_ref, keep_ref, up_ref, left_ref, corner_ref):
    wire = wire_ref[:, :WIDE]
    tokens = x_ref.shape[0]
    both = None
    for k in range(2):
        row = meta_ref[:, 2 + k : 3 + k].astype(jnp.int32)
        masks = wire_masks(row, (tokens, wire.shape[0]), 1)
        both = masks if both is None else tuple(a + b for a, b in zip(both, masks))
    du = jnp.concatenate(from_wire(both, wire), axis=1)
    xhat, r = normalize(x_ref[...])
    dx = r * (
        du
        - jnp.mean(du, axis=-1, keepdims=True)
        - xhat * jnp.mean(du * xhat, axis=-1, keepdims=True)
    )
    ds = (dout_ref[...].astype(jnp.float32) + dx).astype(jnp.bfloat16)
    ds_ref[...] = ds
    keep_ref[...] = ds
    up_ref[...] = ds[: 4 * tc]
    n = 4 * tr
    s = iota((n, 1), 0)
    edge = dot(ones_where((s // 4) * tc + s % 4 == iota((n, tokens), 1)), ds).astype(jnp.bfloat16)
    left_ref[...] = edge
    corner_ref[...] = edge[:16]


def roll_back(tr, tc, off_ref, ds_ref, down_ref, right_ref, corner_ref, out_ref):
    t = iota((ds_ref.shape[0], 1), 0)
    inside, halo = places(t // tc + off_ref[0], t % tc + off_ref[1], tr, tc)
    edge = jnp.concatenate([down_ref[...], right_ref[...], corner_ref[...]], axis=0)
    out_ref[...] = (dot(inside, ds_ref[...]) + dot(halo, edge)).astype(jnp.bfloat16)


def combine_y(wire_ref, meta_ref, x_ref, dout_ref, out_ref, dg_ref):
    wire = wire_ref[:, WIDE:]
    dout = dout_ref[...].astype(jnp.float32)
    tokens = dout.shape[0]
    total = x_ref[...]
    lane = iota((tokens, tokens), 1)
    table = jnp.zeros((tokens, tokens), jnp.float32)
    for k in range(2):
        row = meta_ref[:, 2 + k : 3 + k].astype(jnp.int32)
        y = jnp.concatenate(from_wire(wire_masks(row, (tokens, wire.shape[0]), 1), wire), axis=1)
        total = total + meta_ref[:, k : k + 1] * y
        table = jnp.where(lane == k, jnp.sum(dout * y, axis=-1, keepdims=True), table)
    out_ref[...] = total.astype(jnp.bfloat16)
    dg_ref[...] = table.T[:2]


def exchange(wire, n):
    blocks = wire.reshape(n, WIRE_ROWS, wire.shape[-1])
    out = lax.all_to_all(blocks, "expert", split_axis=0, concat_axis=0, tiled=True)
    return out.reshape(wire.shape)


def edges(row_edge, col_edge, corner, step):
    n_dp, n_ex = lax.axis_size("dp"), lax.axis_size("expert")
    by_dp = [(i, (i + step) % n_dp) for i in range(n_dp)]
    by_ex = [(i, (i + step) % n_ex) for i in range(n_ex)]
    by_both = [
        (q * n_dp + p, (q + step) % n_ex * n_dp + (p + step) % n_dp)
        for q in range(n_ex)
        for p in range(n_dp)
    ]
    return (
        lax.ppermute(row_edge, "dp", by_dp),
        lax.ppermute(col_edge, "expert", by_ex),
        lax.ppermute(corner, ("expert", "dp"), by_both),
    )


def per_device(attn_win, shortcut, d_out, expert_ids, gate_probs, shift_offsets, w_in, w_out):
    tr, tc, width = attn_win.shape
    tokens = tr * tc
    n_ex = lax.axis_size("expert")
    n = n_ex * WIRE_ROWS
    bf16 = functools.partial(jax.ShapeDtypeStruct, dtype=jnp.bfloat16)
    f32 = functools.partial(jax.ShapeDtypeStruct, dtype=jnp.float32)
    ids = expert_ids.reshape(tokens, 2).T
    gates = gate_probs.reshape(tokens, 2).T
    dout = d_out.reshape(tokens, width)
    part = w_out.shape[1]

    up, left, corner, w_own = pl.pallas_call(
        prepare,
        out_shape=(
            bf16((4 * tc, width)),
            bf16((4 * tr, width)),
            bf16((16, width)),
            bf16((1, 2, part, width)),
        ),
        in_specs=[ANY] * 3,
        out_specs=(VMEM,) * 3 + (ANY,),
        scratch_shapes=[pltpu.VMEM((tr, tc, width), jnp.bfloat16), pltpu.SemaphoreType.DMA((3,))],
        compiler_params=pltpu.CompilerParams(vmem_limit_bytes=58 * 1024 * 1024),
        cost_estimate=pl.CostEstimate(flops=1 << 25, bytes_accessed=1 << 21, transcendentals=0),
    )(attn_win, w_in.transpose(0, 2, 1), w_out)
    w_all = lax.all_gather(w_own, "dp", axis=0, tiled=True)
    up, left, corner = edges(up, left, corner, 1)
    g_wire, masks, meta, x0, sel = call(
        functools.partial(dispatch_g, tr, tc),
        (
            bf16((n, WIDE)),
            bf16((3, n, tokens)),
            f32((tokens, tokens)),
            f32((tokens, width)),
            bf16((tokens, 4 * tc + 4 * tr + 16)),
        ),
        shift_offsets, ids, gates, dout, attn_win.reshape(tokens, width), shortcut.reshape(tokens, width),
        specs=[SMEM] + [VMEM] * 5,
        flops=4 * 256 * n * WIDE, traffic=1 << 20,
    )
    sent, x = call(
        dispatch_u,
        (bf16((n, 2 * WIDE)), f32((tokens, width))),
        g_wire, masks, x0, sel, up, left, corner,
        flops=4 * 128 * n * WIDE, traffic=1 << 21,
    )
    returned, grads = experts(exchange(sent, n_ex), w_all)
    returned = exchange(returned, n_ex)
    grad = lax.psum_scatter(grads, "dp", scatter_dimension=0, tiled=True)
    grad_in = grad[:, 0].transpose(0, 2, 1).astype(jnp.float32)
    grad_out = grad[:, 1].astype(jnp.float32)
    ds, ds_keep, up_b, left_b, corner_b = call(
        functools.partial(combine_q, tr, tc),
        (
            bf16((tokens, width)),
            bf16((tokens, width)),
            bf16((4 * tc, width)),
            bf16((4 * tr, width)),
            bf16((16, width)),
        ),
        returned, meta, x, dout,
        flops=4 * tokens * n * WIDE, traffic=1 << 21,
    )
    down, right, corner_r = edges(up_b, left_b, corner_b, -1)
    block_out, d_gates = call(
        combine_y,
        (bf16((tokens, width)), f32((2, tokens))),
        returned, meta, x, dout,
        flops=8 * tokens * n * WIDE, traffic=1 << 21,
    )
    d_attn = call(
        functools.partial(roll_back, tr, tc),
        bf16((tokens, width)),
        shift_offsets, ds_keep, down, right, corner_r,
        specs=[SMEM] + [VMEM] * 4,
        flops=2 * tokens * 256 * width, traffic=1 << 19,
    )
    tile = (tr, tc, width)
    return (
        block_out.reshape(tile),
        ds.reshape(tile),
        d_attn.reshape(tile),
        d_gates.T.reshape(1, 1, tokens, 2),
        grad_in,
        grad_out,
    )


def solution(mesh):
    tile = P("dp", "expert", None)
    pairs = P("dp", "expert", None, None)
    first, second = P("expert", None, "dp"), P("expert", "dp", None)
    return jax.shard_map(
        per_device,
        mesh=mesh,
        in_specs=(tile, tile, tile, pairs, pairs, P(), first, second),
        out_specs=(tile, tile, tile, pairs, first, second),
        check_vma=False,
    )
```

```python
import functools

import jax
import jax.numpy as jnp
from jax import lax
from jax.experimental import pallas as pl
from jax.experimental.pallas import tpu as pltpu
from jax.sharding import PartitionSpec as P

CAP = 5
SPARE = 48 << 20
WIRE_ROWS = 8
WIDE = 512
EPS = 1e-05
VMEM = pl.BlockSpec(memory_space=pltpu.VMEM)
HBM = pl.BlockSpec(memory_space=pltpu.HBM)
SMEM = pl.BlockSpec(memory_space=pltpu.SMEM)


def iota(shape, dim):
    return lax.broadcasted_iota(jnp.int32, shape, dim)


def ones_where(mask):
    return jnp.where(mask, 1.0, 0.0).astype(jnp.bfloat16)


def dot(a, b):
    return jnp.dot(a, b, preferred_element_type=jnp.float32)


def dot_t(a, b):
    return lax.dot_general(a, b, (((1,), (1,)), ((), ())), preferred_element_type=jnp.float32)


def t_dot(a, b):
    return lax.dot_general(a, b, (((0,), (0,)), ((), ())), preferred_element_type=jnp.float32)


def call(body, outs, *args, flops=0, traffic=0, specs=None, **kw):
    return pl.pallas_call(
        body,
        out_shape=outs,
        in_specs=[VMEM] * len(args) if specs is None else specs,
        out_specs=jax.tree.map(lambda _: VMEM, outs),
        compiler_params=pltpu.CompilerParams(vmem_limit_bytes=32 * 1024 * 1024),
        cost_estimate=pl.CostEstimate(flops=flops, bytes_accessed=traffic, transcendentals=0),
        **kw,
    )(*args)


def wire_masks(row, shape, dim):
    at = iota(shape, dim)
    pos = row & 7
    tail = row - pos + CAP + (pos >> 1)
    odd = (pos & 1) == 1
    left = jnp.where(odd, -1, tail)
    right = jnp.where(odd, tail, -1)
    return ones_where(at == row), ones_where(at == left), ones_where(at == right)


def from_wire(masks, wire):
    head, left, right = masks
    half = WIDE // 2
    return (
        dot(head, wire),
        dot(left, wire[:, :half]) + dot(right, wire[:, half:]),
    )


def to_wire(masks, rows, turned):
    head, left, right = masks
    f = t_dot if turned else dot
    tail = rows[:, WIDE:]
    return f(head, rows[:, :WIDE]) + jnp.concatenate([f(left, tail), f(right, tail)], axis=1)


def prepare(attn_hbm, w1_hbm, w2_hbm, up_ref, left_ref, corner_ref, w_ref, attn_s, sems):
    copies = [
        pltpu.make_async_copy(src, dst, sems.at[i])
        for i, (src, dst) in enumerate(
            ((attn_hbm, attn_s), (w1_hbm, w_ref.at[:, 0]), (w2_hbm, w_ref.at[:, 1]))
        )
    ]
    for copy in copies:
        copy.start()
    tr, tc, width = attn_s.shape
    tokens = tr * tc
    n = 4 * tr
    s = iota((n, 1), 0)
    edge = ones_where((s // 4) * tc + tc - 4 + s % 4 == iota((n, tokens), 1))
    copies[0].wait()
    attn = attn_s[...].reshape(tokens, width)
    up_ref[...] = attn[tokens - 4 * tc :]
    left = dot(edge, attn).astype(jnp.bfloat16)
    left_ref[...] = left
    corner_ref[...] = left[n - 16 :]
    copies[1].wait()
    copies[2].wait()


def dispatch_g(tr, tc, off_ref, ids_ref, gates_ref, dout_ref, attn_ref, short_ref, sent_ref, mask_ref, meta_ref, x_ref, sel_ref):
    tokens = dout_ref.shape[0]
    t = iota((tokens, 1), 0)
    inside, halo = places(t // tc - off_ref[0], t % tc - off_ref[1], tr, tc)
    sel_ref[...] = halo
    x_ref[...] = short_ref[...].astype(jnp.float32) + dot(inside, attn_ref[...])
    n = sent_ref.shape[0]
    experts = n // WIRE_ROWS
    ids = ids_ref[...]
    rank = iota((experts, tokens), 0)
    first = jnp.where(ids[0:1] == rank, 1.0, 0.0)
    second = jnp.where(ids[1:2] == rank, 1.0, 0.0)
    earlier = ones_where(iota((tokens, tokens), 0) < iota((tokens, tokens), 1))
    before = dot((first + second).astype(jnp.bfloat16), earlier)
    row0 = ids[0:1] * WIRE_ROWS + jnp.sum(before * first, axis=0, keepdims=True).astype(jnp.int32)
    row1 = ids[1:2] * WIRE_ROWS + jnp.sum(before * second, axis=0, keepdims=True).astype(jnp.int32)
    at = iota((tokens, tokens), 0)
    table = jnp.where(at == 0, gates_ref[0:1], 0.0)
    table = jnp.where(at == 1, gates_ref[1:2], table)
    table = jnp.where(at == 2, row0.astype(jnp.float32), table)
    table = jnp.where(at == 3, row1.astype(jnp.float32), table)
    meta = table.T
    meta_ref[...] = meta
    dout = dout_ref[...].astype(jnp.float32)
    sent = 0.0
    both = None
    for k, row in enumerate((row0, row1)):
        masks = wire_masks(row, (n, tokens), 0)
        sent = sent + to_wire(masks, (meta[:, k : k + 1] * dout).astype(jnp.bfloat16), False)
        both = masks if both is None else tuple(a + b for a, b in zip(both, masks))
    for m in range(3):
        mask_ref[m] = both[m]
    sent_ref[...] = sent.astype(jnp.bfloat16)


def normalize(x):
    m = jnp.mean(x, axis=-1, keepdims=True)
    c = x - m
    r = lax.rsqrt(jnp.mean(c * c, axis=-1, keepdims=True) + EPS)
    return c * r, r


def places(i, j, tr, tc):
    tokens = i.shape[0]
    i_in = (i >= 0) & (i < tr)
    j_in = (j >= 0) & (j < tc)
    ei = jnp.where(i < 0, i + 4, i - tr)
    ej = jnp.where(j < 0, j + 4, j - tc)
    own = jnp.where(i_in & j_in, i * tc + j, -1)
    edge = jnp.where(
        i_in,
        jnp.where(j_in, -1, 4 * tc + i * 4 + ej),
        jnp.where(j_in, ei * tc + j, 4 * tc + 4 * tr + ei * 4 + ej),
    )
    count = 4 * tc + 4 * tr + 16
    return (
        ones_where(own == iota((tokens, tokens), 1)),
        ones_where(edge == iota((tokens, count), 1)),
    )


def dispatch_u(g_ref, mask_ref, x0_ref, sel_ref, up_ref, left_ref, corner_ref, sent_ref, x_ref):
    edge = jnp.concatenate([up_ref[...], left_ref[...], corner_ref[...]], axis=0)
    x = x0_ref[...] + dot(sel_ref[...], edge)
    x_ref[...] = x
    xhat, _ = normalize(x)
    masks = tuple(mask_ref[m] for m in range(3))
    sent_ref[:, :WIDE] = g_ref[...]
    sent_ref[:, WIDE:] = to_wire(masks, xhat.astype(jnp.bfloat16), False).astype(jnp.bfloat16)


def slot_masks(dim, peers):
    slots = peers * CAP
    s = iota((slots, 1) if dim else (1, slots), 1 - dim)
    row = (s % peers) * WIRE_ROWS + s // peers
    wire = peers * WIRE_ROWS
    return wire_masks(row, (slots, wire) if dim else (wire, slots), dim)


def experts_body(wire_ref, w_hbm, out_ref, grad_hbm, w_s, grad_s, u_s, g_s, in_sems, out_sems):
    parts, _, part, width = w_s.shape
    half = parts // 2
    hidden = half * part
    pieces = [(c, k) for c in range(2) for k in range(2)]
    ins = [
        pltpu.make_async_copy(
            w_hbm.at[pl.ds(c * half, half), k], w_s.at[pl.ds(c * half, half), k], in_sems.at[i]
        )
        for i, (c, k) in enumerate(pieces)
    ]
    outs = [
        pltpu.make_async_copy(
            grad_s.at[pl.ds(c * half, half), k], grad_hbm.at[pl.ds(c * half, half), k], out_sems.at[i]
        )
        for i, (c, k) in enumerate(pieces)
    ]
    for copy in ins:
        copy.start()
    n = wire_ref.shape[0]
    peers = min(32, n // WIRE_ROWS)
    rows, slots = peers * WIRE_ROWS, peers * CAP
    blocks = n // rows
    masks = slot_masks(1, peers)
    for b in range(blocks):
        for at, dst in ((0, g_s), (WIDE, u_s)):
            head, tail = from_wire(masks, wire_ref[b * rows : (b + 1) * rows, at : at + WIDE])
            dst[b * slots : (b + 1) * slots, :WIDE] = head.astype(jnp.bfloat16)
            dst[b * slots : (b + 1) * slots, WIDE:] = tail.astype(jnp.bfloat16)
    u = u_s[...]
    g = g_s[...]

    def weights(c, k):
        return w_s[c * half : (c + 1) * half, k].reshape(hidden, width)

    pairs = []
    for c in range(2):
        ins[2 * c].wait()
        h = dot_t(u, weights(c, 0))
        ins[2 * c + 1].wait()
        pairs.append((h, dot_t(g, weights(c, 1))))
    acts = []
    for c, (h, da) in enumerate(pairs):
        cdf = 0.5 * (1.0 + lax.erf(h * 0.7071067811865476))
        pdf = jnp.exp(-0.5 * h * h) * 0.3989422804014327
        a = (h * cdf).astype(jnp.bfloat16)
        p = (da * (cdf + h * pdf)).astype(jnp.bfloat16)
        acts.append((p, a))
        for k, (left, right) in enumerate(((p, u), (a, g))):
            grad = t_dot(left, right).astype(jnp.bfloat16)
            grad_s[c * half : (c + 1) * half, k] = grad.reshape(half, part, width)
            outs[2 * c + k].start()
    q = dot(acts[0][0], weights(0, 0)) + dot(acts[1][0], weights(1, 0))
    y = dot(acts[0][1], weights(0, 1)) + dot(acts[1][1], weights(1, 1))
    masks = slot_masks(0, peers)
    for at, src in ((0, q.astype(jnp.bfloat16)), (WIDE, y.astype(jnp.bfloat16))):
        for b in range(blocks):
            block = to_wire(masks, src[b * slots : (b + 1) * slots], False)
            out_ref[b * rows : (b + 1) * rows, at : at + WIDE] = block.astype(jnp.bfloat16)
    for copy in outs:
        copy.wait()


def experts(wire, w):
    n = wire.shape[0]
    parts, _, part, width = w.shape
    slots = n // WIRE_ROWS * CAP
    hidden = parts * part
    return pl.pallas_call(
        experts_body,
        out_shape=(
            jax.ShapeDtypeStruct((n, 2 * WIDE), jnp.bfloat16),
            jax.ShapeDtypeStruct(w.shape, jnp.bfloat16),
        ),
        in_specs=[VMEM, HBM],
        out_specs=(VMEM, HBM),
        scratch_shapes=[
            pltpu.VMEM(w.shape, jnp.bfloat16),
            pltpu.VMEM(w.shape, jnp.bfloat16),
            pltpu.VMEM((slots, width), jnp.bfloat16),
            pltpu.VMEM((slots, width), jnp.bfloat16),
            pltpu.SemaphoreType.DMA((4,)),
            pltpu.SemaphoreType.DMA((4,)),
        ],
        compiler_params=pltpu.CompilerParams(vmem_limit_bytes=SPARE),
        cost_estimate=pl.CostEstimate(
            flops=12 * slots * hidden * width,
            bytes_accessed=8 * hidden * width,
            transcendentals=2 * slots * hidden,
        ),
    )(wire, w)


def combine_q(tr, tc, wire_ref, meta_ref, x_ref, dout_ref, ds_ref, keep_ref, up_ref, left_ref, corner_ref):
    wire = wire_ref[:, :WIDE]
    tokens = x_ref.shape[0]
    both = None
    for k in range(2):
        row = meta_ref[:, 2 + k : 3 + k].astype(jnp.int32)
        masks = wire_masks(row, (tokens, wire.shape[0]), 1)
        both = masks if both is None else tuple(a + b for a, b in zip(both, masks))
    du = jnp.concatenate(from_wire(both, wire), axis=1)
    xhat, r = normalize(x_ref[...])
    dx = r * (
        du
        - jnp.mean(du, axis=-1, keepdims=True)
        - xhat * jnp.mean(du * xhat, axis=-1, keepdims=True)
    )
    ds = (dout_ref[...].astype(jnp.float32) + dx).astype(jnp.bfloat16)
    ds_ref[...] = ds
    keep_ref[...] = ds
    up_ref[...] = ds[: 4 * tc]
    n = 4 * tr
    s = iota((n, 1), 0)
    edge = dot(ones_where((s // 4) * tc + s % 4 == iota((n, tokens), 1)), ds).astype(jnp.bfloat16)
    left_ref[...] = edge
    corner_ref[...] = edge[:16]


def roll_back(tr, tc, off_ref, ds_ref, down_ref, right_ref, corner_ref, out_ref):
    t = iota((ds_ref.shape[0], 1), 0)
    inside, halo = places(t // tc + off_ref[0], t % tc + off_ref[1], tr, tc)
    edge = jnp.concatenate([down_ref[...], right_ref[...], corner_ref[...]], axis=0)
    out_ref[...] = (dot(inside, ds_ref[...]) + dot(halo, edge)).astype(jnp.bfloat16)


def combine_y(wire_ref, meta_ref, x_ref, dout_ref, out_ref, dg_ref):
    wire = wire_ref[:, WIDE:]
    dout = dout_ref[...].astype(jnp.float32)
    tokens = dout.shape[0]
    total = x_ref[...]
    lane = iota((tokens, tokens), 1)
    table = jnp.zeros((tokens, tokens), jnp.float32)
    for k in range(2):
        row = meta_ref[:, 2 + k : 3 + k].astype(jnp.int32)
        y = jnp.concatenate(from_wire(wire_masks(row, (tokens, wire.shape[0]), 1), wire), axis=1)
        total = total + meta_ref[:, k : k + 1] * y
        table = jnp.where(lane == k, jnp.sum(dout * y, axis=-1, keepdims=True), table)
    out_ref[...] = total.astype(jnp.bfloat16)
    dg_ref[...] = table.T[:2]


def exchange(wire, n):
    blocks = wire.reshape(n, WIRE_ROWS, wire.shape[-1])
    out = lax.all_to_all(blocks, "expert", split_axis=0, concat_axis=0, tiled=True)
    return out.reshape(wire.shape)


def edges(row_edge, col_edge, corner, step):
    n_dp, n_ex = lax.axis_size("dp"), lax.axis_size("expert")
    by_dp = [(i, (i + step) % n_dp) for i in range(n_dp)]
    by_ex = [(i, (i + step) % n_ex) for i in range(n_ex)]
    by_both = [
        (q * n_dp + p, (q + step) % n_ex * n_dp + (p + step) % n_dp)
        for q in range(n_ex)
        for p in range(n_dp)
    ]
    return (
        lax.ppermute(row_edge, "dp", by_dp),
        lax.ppermute(col_edge, "expert", by_ex),
        lax.ppermute(corner, ("expert", "dp"), by_both),
    )


def per_device(attn_win, shortcut, d_out, expert_ids, gate_probs, shift_offsets, w_in, w_out):
    tr, tc, width = attn_win.shape
    tokens = tr * tc
    n_ex = lax.axis_size("expert")
    n = n_ex * WIRE_ROWS
    bf16 = functools.partial(jax.ShapeDtypeStruct, dtype=jnp.bfloat16)
    f32 = functools.partial(jax.ShapeDtypeStruct, dtype=jnp.float32)
    ids = expert_ids.reshape(tokens, 2).T
    gates = gate_probs.reshape(tokens, 2).T
    dout = d_out.reshape(tokens, width)
    part = w_out.shape[1]

    up, left, corner, w_own = pl.pallas_call(
        prepare,
        out_shape=(
            bf16((4 * tc, width)),
            bf16((4 * tr, width)),
            bf16((16, width)),
            bf16((1, 2, part, width)),
        ),
        in_specs=[HBM] * 3,
        out_specs=(VMEM,) * 4,
        scratch_shapes=[pltpu.VMEM((tr, tc, width), jnp.bfloat16), pltpu.SemaphoreType.DMA((3,))],
        compiler_params=pltpu.CompilerParams(vmem_limit_bytes=58 << 20),
        cost_estimate=pl.CostEstimate(flops=1 << 25, bytes_accessed=1 << 21, transcendentals=0),
    )(attn_win, w_in.transpose(0, 2, 1), w_out)
    w_all = lax.all_gather(w_own, "dp", axis=0, tiled=True)
    up, left, corner = edges(up, left, corner, 1)
    g_wire, masks, meta, x0, sel = call(
        functools.partial(dispatch_g, tr, tc),
        (
            bf16((n, WIDE)),
            bf16((3, n, tokens)),
            f32((tokens, tokens)),
            f32((tokens, width)),
            bf16((tokens, 4 * tc + 4 * tr + 16)),
        ),
        shift_offsets, ids, gates, dout, attn_win.reshape(tokens, width), shortcut.reshape(tokens, width),
        specs=[SMEM] + [VMEM] * 5,
        flops=4 * 256 * n * WIDE, traffic=1 << 20,
    )
    sent, x = call(
        dispatch_u,
        (bf16((n, 2 * WIDE)), f32((tokens, width))),
        g_wire, masks, x0, sel, up, left, corner,
        flops=4 * 128 * n * WIDE, traffic=1 << 21,
    )
    returned, grads = experts(exchange(sent, n_ex), w_all)
    returned = exchange(returned, n_ex)
    grad = lax.psum_scatter(grads, "dp", scatter_dimension=0, tiled=True)
    grad_in = grad[:, 0].transpose(0, 2, 1).astype(jnp.float32)
    grad_out = grad[:, 1].astype(jnp.float32)
    ds, ds_keep, up_b, left_b, corner_b = call(
        functools.partial(combine_q, tr, tc),
        (
            bf16((tokens, width)),
            bf16((tokens, width)),
            bf16((4 * tc, width)),
            bf16((4 * tr, width)),
            bf16((16, width)),
        ),
        returned, meta, x, dout,
        flops=4 * tokens * n * WIDE, traffic=1 << 21,
    )
    down, right, corner_r = edges(up_b, left_b, corner_b, -1)
    block_out, d_gates = call(
        combine_y,
        (bf16((tokens, width)), f32((2, tokens))),
        returned, meta, x, dout,
        flops=8 * tokens * n * WIDE, traffic=1 << 21,
    )
    d_attn = call(
        functools.partial(roll_back, tr, tc),
        bf16((tokens, width)),
        shift_offsets, ds_keep, down, right, corner_r,
        specs=[SMEM] + [VMEM] * 4,
        flops=2 * tokens * 256 * width, traffic=1 << 19,
    )
    tile = (tr, tc, width)
    return (
        block_out.reshape(tile),
        ds.reshape(tile),
        d_attn.reshape(tile),
        d_gates.T.reshape(1, 1, tokens, 2),
        grad_in,
        grad_out,
    )


def solution(mesh):
    tile = P("dp", "expert", None)
    pairs = P("dp", "expert", None, None)
    first, second = P("expert", None, "dp"), P("expert", "dp", None)
    return jax.shard_map(
        per_device,
        mesh=mesh,
        in_specs=(tile, tile, tile, pairs, pairs, P(), first, second),
        out_specs=(tile, tile, tile, pairs, first, second),
        check_vma=False,
    )
```

```python
import functools

import jax
import jax.numpy as jnp
from jax import lax
from jax.experimental import pallas as pl
from jax.experimental.pallas import tpu as pltpu
from jax.sharding import PartitionSpec as P

CAP = 5
WIRE_ROWS = 8
WIDE = 512
EPS = 1e-05
VMEM = pl.BlockSpec(memory_space=pltpu.VMEM)
ANY = pl.BlockSpec(memory_space=pl.ANY)
SMEM = pl.BlockSpec(memory_space=pltpu.SMEM)


def iota(shape, dim):
    return lax.broadcasted_iota(jnp.int32, shape, dim)


def ones_where(mask):
    return jnp.where(mask, 1.0, 0.0).astype(jnp.bfloat16)


def dot(a, b):
    return jnp.dot(a, b, preferred_element_type=jnp.float32)


def dot_t(a, b):
    return lax.dot_general(a, b, (((1,), (1,)), ((), ())), preferred_element_type=jnp.float32)


def t_dot(a, b):
    return lax.dot_general(a, b, (((0,), (0,)), ((), ())), preferred_element_type=jnp.float32)


def in_hbm(x):
    return pltpu.with_memory_space_constraint(x, pltpu.HBM)


def call(body, outs, *args, flops=0, traffic=0, specs=None, **kw):
    return pl.pallas_call(
        body,
        out_shape=outs,
        in_specs=[VMEM] * len(args) if specs is None else specs,
        out_specs=jax.tree.map(lambda _: VMEM, outs),
        compiler_params=pltpu.CompilerParams(vmem_limit_bytes=32 * 1024 * 1024),
        cost_estimate=pl.CostEstimate(flops=flops, bytes_accessed=traffic, transcendentals=0),
        **kw,
    )(*args)


def wire_masks(row, shape, dim):
    at = iota(shape, dim)
    pos = row & 7
    tail = row - pos + CAP + (pos >> 1)
    odd = (pos & 1) == 1
    left = jnp.where(odd, -1, tail)
    right = jnp.where(odd, tail, -1)
    return ones_where(at == row), ones_where(at == left), ones_where(at == right)


def from_wire(masks, wire):
    head, left, right = masks
    half = WIDE // 2
    return (
        dot(head, wire),
        dot(left, wire[:, :half]) + dot(right, wire[:, half:]),
    )


def to_wire(masks, rows, turned):
    head, left, right = masks
    f = t_dot if turned else dot
    tail = rows[:, WIDE:]
    return f(head, rows[:, :WIDE]) + jnp.concatenate([f(left, tail), f(right, tail)], axis=1)


def prepare(attn_hbm, w1_hbm, w2_hbm, up_ref, left_ref, corner_ref, w_ref, attn_s, sems):
    copies = [
        pltpu.make_async_copy(src, dst, sems.at[i])
        for i, (src, dst) in enumerate(
            ((attn_hbm, attn_s), (w1_hbm, w_ref.at[:, 0]), (w2_hbm, w_ref.at[:, 1]))
        )
    ]
    for copy in copies:
        copy.start()
    tr, tc, width = attn_s.shape
    tokens = tr * tc
    n = 4 * tr
    s = iota((n, 1), 0)
    edge = ones_where((s // 4) * tc + tc - 4 + s % 4 == iota((n, tokens), 1))
    copies[0].wait()
    attn = attn_s[...].reshape(tokens, width)
    up_ref[...] = attn[tokens - 4 * tc :]
    left = dot(edge, attn).astype(jnp.bfloat16)
    left_ref[...] = left
    corner_ref[...] = left[n - 16 :]
    copies[1].wait()
    copies[2].wait()


def dispatch_g(
    off_hbm, ids_hbm, gates_hbm, dout_hbm, attn_hbm, short_hbm,
    sent_ref, mask_ref, meta_ref, x_ref, sel_ref,
    off_ref, ids_ref, gates_ref, dout_s, attn_s, short_s, sems,
):
    copies = [
        pltpu.make_async_copy(src, dst, sems.at[i])
        for i, (src, dst) in enumerate(
            (
                (off_hbm, off_ref),
                (ids_hbm, ids_ref),
                (gates_hbm, gates_ref),
                (attn_hbm, attn_s),
                (short_hbm, short_s),
                (dout_hbm, dout_s),
            )
        )
    ]
    for copy in copies:
        copy.start()
    for copy in copies:
        copy.wait()
    tr, tc, width = attn_s.shape
    tokens = tr * tc
    t = iota((tokens, 1), 0)
    inside, halo = places(t // tc - off_ref[0], t % tc - off_ref[1], tr, tc)
    sel_ref[...] = halo
    x_ref[...] = short_s[...].reshape(tokens, width).astype(jnp.float32) + dot(
        inside, attn_s[...].reshape(tokens, width)
    )
    n = sent_ref.shape[0]
    experts = n // WIRE_ROWS
    ids = ids_ref[...]
    rank = iota((experts, tokens), 0)
    first = jnp.where(ids[0:1] == rank, 1.0, 0.0)
    second = jnp.where(ids[1:2] == rank, 1.0, 0.0)
    earlier = ones_where(iota((tokens, tokens), 0) < iota((tokens, tokens), 1))
    before = dot((first + second).astype(jnp.bfloat16), earlier)
    row0 = ids[0:1] * WIRE_ROWS + jnp.sum(before * first, axis=0, keepdims=True).astype(jnp.int32)
    row1 = ids[1:2] * WIRE_ROWS + jnp.sum(before * second, axis=0, keepdims=True).astype(jnp.int32)
    at = iota((tokens, tokens), 0)
    table = jnp.where(at == 0, gates_ref[0:1], 0.0)
    table = jnp.where(at == 1, gates_ref[1:2], table)
    table = jnp.where(at == 2, row0.astype(jnp.float32), table)
    table = jnp.where(at == 3, row1.astype(jnp.float32), table)
    meta = table.T
    meta_ref[...] = meta
    dout = dout_s[...].reshape(tokens, width).astype(jnp.float32)
    sent = 0.0
    both = None
    for k, row in enumerate((row0, row1)):
        masks = wire_masks(row, (n, tokens), 0)
        sent = sent + to_wire(masks, (meta[:, k : k + 1] * dout).astype(jnp.bfloat16), False)
        both = masks if both is None else tuple(a + b for a, b in zip(both, masks))
    for m in range(3):
        mask_ref[m] = both[m]
    sent_ref[...] = sent.astype(jnp.bfloat16)


def normalize(x):
    m = jnp.mean(x, axis=-1, keepdims=True)
    c = x - m
    r = lax.rsqrt(jnp.mean(c * c, axis=-1, keepdims=True) + EPS)
    return c * r, r


def places(i, j, tr, tc):
    tokens = i.shape[0]
    i_in = (i >= 0) & (i < tr)
    j_in = (j >= 0) & (j < tc)
    ei = jnp.where(i < 0, i + 4, i - tr)
    ej = jnp.where(j < 0, j + 4, j - tc)
    own = jnp.where(i_in & j_in, i * tc + j, -1)
    edge = jnp.where(
        i_in,
        jnp.where(j_in, -1, 4 * tc + i * 4 + ej),
        jnp.where(j_in, ei * tc + j, 4 * tc + 4 * tr + ei * 4 + ej),
    )
    count = 4 * tc + 4 * tr + 16
    return (
        ones_where(own == iota((tokens, tokens), 1)),
        ones_where(edge == iota((tokens, count), 1)),
    )


def dispatch_u(g_ref, mask_ref, x0_ref, sel_ref, up_ref, left_ref, corner_ref, sent_ref, x_ref):
    edge = jnp.concatenate([up_ref[...], left_ref[...], corner_ref[...]], axis=0)
    x = x0_ref[...] + dot(sel_ref[...], edge)
    x_ref[...] = x
    xhat, _ = normalize(x)
    masks = tuple(mask_ref[m] for m in range(3))
    sent_ref[:, :WIDE] = g_ref[...]
    sent_ref[:, WIDE:] = to_wire(masks, xhat.astype(jnp.bfloat16), False).astype(jnp.bfloat16)


def slot_masks(dim, peers):
    slots = peers * CAP
    s = iota((slots, 1) if dim else (1, slots), 1 - dim)
    row = (s % peers) * WIRE_ROWS + s // peers
    wire = peers * WIRE_ROWS
    return wire_masks(row, (slots, wire) if dim else (wire, slots), dim)


def backward_body(
    wire_ref, w_hbm, out_ref, u_hbm, g_hbm, a_ref, p_ref, w_s, u_ref, g_ref, sems, keep_sems
):
    parts, _, part, width = w_s.shape
    half = parts // 2
    hidden = half * part
    copies = [
        pltpu.make_async_copy(
            w_hbm.at[pl.ds(c * half, half), k], w_s.at[pl.ds(c * half, half), k], sems.at[2 * c + k]
        )
        for c in range(2)
        for k in range(2)
    ]
    for copy in copies:
        copy.start()
    n = wire_ref.shape[0]
    peers = min(32, n // WIRE_ROWS)
    rows, slots = peers * WIRE_ROWS, peers * CAP
    blocks = n // rows
    masks = slot_masks(1, peers)
    for b in range(blocks):
        for at, dst in ((0, g_ref), (WIDE, u_ref)):
            head, tail = from_wire(masks, wire_ref[b * rows : (b + 1) * rows, at : at + WIDE])
            dst[b * slots : (b + 1) * slots, :WIDE] = head.astype(jnp.bfloat16)
            dst[b * slots : (b + 1) * slots, WIDE:] = tail.astype(jnp.bfloat16)
    keep = [
        pltpu.make_async_copy(u_ref, u_hbm, keep_sems.at[0]),
        pltpu.make_async_copy(g_ref, g_hbm, keep_sems.at[1]),
    ]
    for copy in keep:
        copy.start()
    u = u_ref[...]
    g = g_ref[...]

    def weights(c, k):
        return w_s[c * half : (c + 1) * half, k].reshape(hidden, width)

    pairs = []
    for c in range(2):
        copies[2 * c].wait()
        h = dot_t(u, weights(c, 0))
        copies[2 * c + 1].wait()
        pairs.append((h, dot_t(g, weights(c, 1))))
    q = None
    for c, (h, da) in enumerate(pairs):
        cdf = 0.5 * (1.0 + lax.erf(h * 0.7071067811865476))
        pdf = jnp.exp(-0.5 * h * h) * 0.3989422804014327
        p = (da * (cdf + h * pdf)).astype(jnp.bfloat16)
        a_ref[:, c * hidden : (c + 1) * hidden] = (h * cdf).astype(jnp.bfloat16)
        p_ref[:, c * hidden : (c + 1) * hidden] = p
        q_c = dot(p, weights(c, 0))
        q = q_c if q is None else q + q_c
    send_slots(q.astype(jnp.bfloat16), out_ref)
    for copy in keep:
        copy.wait()


def send_slots(rows_of, out_ref):
    n = out_ref.shape[0]
    peers = min(32, n // WIRE_ROWS)
    rows, slots = peers * WIRE_ROWS, peers * CAP
    masks = slot_masks(0, peers)
    for b in range(n // rows):
        block = to_wire(masks, rows_of[b * slots : (b + 1) * slots], False)
        out_ref[b * rows : (b + 1) * rows] = block.astype(jnp.bfloat16)


def forward_body(a_ref, w_hbm, out_ref, w_s, sem):
    parts, part, width = w_s.shape
    fetch = pltpu.make_async_copy(w_hbm.at[:, 1], w_s, sem)
    fetch.start()
    fetch.wait()
    y = dot(a_ref[...], w_s[...].reshape(parts * part, width))
    send_slots(y.astype(jnp.bfloat16), out_ref)


def gradients_body(u_hbm, g_hbm, a_ref, p_ref, grad_hbm, grad_s, u_ref, g_ref, sems, in_sems):
    parts, _, part, width = grad_s.shape
    half = parts // 2
    hidden = half * part
    ins = [
        pltpu.make_async_copy(u_hbm, u_ref, in_sems.at[0]),
        pltpu.make_async_copy(g_hbm, g_ref, in_sems.at[1]),
    ]
    for copy in ins:
        copy.start()
    for copy in ins:
        copy.wait()
    outs = []
    for c in range(2):
        for k, (left, right) in enumerate(((p_ref, u_ref), (a_ref, g_ref))):
            grad = t_dot(left[:, c * hidden : (c + 1) * hidden], right[...]).astype(jnp.bfloat16)
            at = pl.ds(c * half, half)
            grad_s[c * half : (c + 1) * half, k] = grad.reshape(half, part, width)
            outs.append(pltpu.make_async_copy(grad_s.at[at, k], grad_hbm.at[at, k], sems.at[2 * c + k]))
            outs[-1].start()
    for copy in outs:
        copy.wait()


def widen(grad_hbm, first_hbm, second_hbm, grad_s, wide_s, sems):
    outs = (first_hbm, second_hbm)
    fetch = [pltpu.make_async_copy(grad_hbm.at[:, k], grad_s.at[:, k], sems.at[k]) for k in range(2)]
    store = [pltpu.make_async_copy(wide_s.at[:, k], outs[k], sems.at[2 + k]) for k in range(2)]
    for copy in fetch:
        copy.start()
    for k in range(2):
        fetch[k].wait()
        wide_s[:, k] = grad_s[:, k].astype(jnp.float32)
        store[k].start()
    for copy in store:
        copy.wait()


def experts(wire, w):
    n = wire.shape[0]
    parts, _, part, width = w.shape
    slots = n // WIRE_ROWS * CAP
    hidden = parts * part
    bf16 = functools.partial(jax.ShapeDtypeStruct, dtype=jnp.bfloat16)
    w = in_hbm(w)
    q_wire, u, g, a, p = pl.pallas_call(
        backward_body,
        out_shape=(
            bf16((n, WIDE)),
            pltpu.HBM((slots, width), jnp.bfloat16),
            pltpu.HBM((slots, width), jnp.bfloat16),
            bf16((slots, hidden)),
            bf16((slots, hidden)),
        ),
        in_specs=[VMEM, ANY],
        out_specs=(VMEM, ANY, ANY, VMEM, VMEM),
        scratch_shapes=[
            pltpu.VMEM(w.shape, jnp.bfloat16),
            pltpu.VMEM((slots, width), jnp.bfloat16),
            pltpu.VMEM((slots, width), jnp.bfloat16),
            pltpu.SemaphoreType.DMA((4,)),
            pltpu.SemaphoreType.DMA((2,)),
        ],
        compiler_params=pltpu.CompilerParams(vmem_limit_bytes=40 << 20),
        cost_estimate=pl.CostEstimate(
            flops=6 * slots * hidden * width,
            bytes_accessed=4 * hidden * width,
            transcendentals=2 * slots * hidden,
        ),
    )(wire, w)
    grads = pl.pallas_call(
        gradients_body,
        out_shape=pltpu.HBM(w.shape, jnp.bfloat16),
        in_specs=[ANY, ANY, VMEM, VMEM],
        out_specs=ANY,
        scratch_shapes=[
            pltpu.VMEM(w.shape, jnp.bfloat16),
            pltpu.VMEM((slots, width), jnp.bfloat16),
            pltpu.VMEM((slots, width), jnp.bfloat16),
            pltpu.SemaphoreType.DMA((4,)),
            pltpu.SemaphoreType.DMA((2,)),
        ],
        compiler_params=pltpu.CompilerParams(vmem_limit_bytes=40 << 20),
        cost_estimate=pl.CostEstimate(
            flops=4 * slots * hidden * width, bytes_accessed=4 * hidden * width, transcendentals=0
        ),
    )(in_hbm(u), in_hbm(g), a, p)
    a, grads = lax.optimization_barrier((a, grads))
    y_wire = pl.pallas_call(
        forward_body,
        out_shape=bf16((n, WIDE)),
        in_specs=[VMEM, ANY],
        out_specs=VMEM,
        scratch_shapes=[pltpu.VMEM((parts, part, width), jnp.bfloat16), pltpu.SemaphoreType.DMA],
        compiler_params=pltpu.CompilerParams(vmem_limit_bytes=40 << 20),
        cost_estimate=pl.CostEstimate(
            flops=2 * slots * hidden * width, bytes_accessed=2 * hidden * width, transcendentals=0
        ),
    )(a, w)
    return q_wire, y_wire, grads


def combine_q(tr, tc, wire_ref, meta_ref, x_ref, dout_ref, ds_ref, keep_ref, up_ref, left_ref, corner_ref):
    wire = wire_ref[...]
    tokens = x_ref.shape[0]
    both = None
    for k in range(2):
        row = meta_ref[:, 2 + k : 3 + k].astype(jnp.int32)
        masks = wire_masks(row, (tokens, wire.shape[0]), 1)
        both = masks if both is None else tuple(a + b for a, b in zip(both, masks))
    du = jnp.concatenate(from_wire(both, wire), axis=1)
    xhat, r = normalize(x_ref[...])
    dx = r * (
        du
        - jnp.mean(du, axis=-1, keepdims=True)
        - xhat * jnp.mean(du * xhat, axis=-1, keepdims=True)
    )
    ds = (dout_ref[...].astype(jnp.float32) + dx).astype(jnp.bfloat16)
    ds_ref[...] = ds
    keep_ref[...] = ds
    up_ref[...] = ds[: 4 * tc]
    n = 4 * tr
    s = iota((n, 1), 0)
    edge = dot(ones_where((s // 4) * tc + s % 4 == iota((n, tokens), 1)), ds).astype(jnp.bfloat16)
    left_ref[...] = edge
    corner_ref[...] = edge[:16]


def roll_back(tr, tc, off_ref, ds_ref, down_ref, right_ref, corner_ref, out_ref):
    t = iota((ds_ref.shape[0], 1), 0)
    inside, halo = places(t // tc + off_ref[0], t % tc + off_ref[1], tr, tc)
    edge = jnp.concatenate([down_ref[...], right_ref[...], corner_ref[...]], axis=0)
    out_ref[...] = (dot(inside, ds_ref[...]) + dot(halo, edge)).astype(jnp.bfloat16)


def combine_y(wire_ref, meta_ref, x_ref, dout_ref, out_ref, dg_ref):
    wire = wire_ref[...]
    dout = dout_ref[...].astype(jnp.float32)
    tokens = dout.shape[0]
    total = x_ref[...]
    lane = iota((tokens, tokens), 1)
    table = jnp.zeros((tokens, tokens), jnp.float32)
    for k in range(2):
        row = meta_ref[:, 2 + k : 3 + k].astype(jnp.int32)
        y = jnp.concatenate(from_wire(wire_masks(row, (tokens, wire.shape[0]), 1), wire), axis=1)
        total = total + meta_ref[:, k : k + 1] * y
        table = jnp.where(lane == k, jnp.sum(dout * y, axis=-1, keepdims=True), table)
    out_ref[...] = total.astype(jnp.bfloat16)
    dg_ref[...] = table.T[:2]


def exchange(wire, n):
    blocks = wire.reshape(n, WIRE_ROWS, wire.shape[-1])
    out = lax.all_to_all(blocks, "expert", split_axis=0, concat_axis=0, tiled=True)
    return out.reshape(wire.shape)


def edges(row_edge, col_edge, corner, step):
    n_dp, n_ex = lax.axis_size("dp"), lax.axis_size("expert")
    by_dp = [(i, (i + step) % n_dp) for i in range(n_dp)]
    by_ex = [(i, (i + step) % n_ex) for i in range(n_ex)]
    by_both = [
        (q * n_dp + p, (q + step) % n_ex * n_dp + (p + step) % n_dp)
        for q in range(n_ex)
        for p in range(n_dp)
    ]
    return (
        lax.ppermute(row_edge, "dp", by_dp),
        lax.ppermute(col_edge, "expert", by_ex),
        lax.ppermute(corner, ("expert", "dp"), by_both),
    )


def per_device(attn_win, shortcut, d_out, expert_ids, gate_probs, shift_offsets, w_in, w_out):
    tr, tc, width = attn_win.shape
    tokens = tr * tc
    n_ex = lax.axis_size("expert")
    n = n_ex * WIRE_ROWS
    bf16 = functools.partial(jax.ShapeDtypeStruct, dtype=jnp.bfloat16)
    f32 = functools.partial(jax.ShapeDtypeStruct, dtype=jnp.float32)
    ids = expert_ids.reshape(tokens, 2).T
    gates = gate_probs.reshape(tokens, 2).T
    dout = d_out.reshape(tokens, width)
    part = w_out.shape[1]

    up, left, corner, w_own = pl.pallas_call(
        prepare,
        out_shape=(
            bf16((4 * tc, width)),
            bf16((4 * tr, width)),
            bf16((16, width)),
            bf16((1, 2, part, width)),
        ),
        in_specs=[ANY] * 3,
        out_specs=(VMEM,) * 4,
        scratch_shapes=[pltpu.VMEM((tr, tc, width), jnp.bfloat16), pltpu.SemaphoreType.DMA((3,))],
        compiler_params=pltpu.CompilerParams(vmem_limit_bytes=32 * 1024 * 1024),
        cost_estimate=pl.CostEstimate(flops=1 << 25, bytes_accessed=1 << 21, transcendentals=0),
    )(in_hbm(attn_win), in_hbm(w_in.transpose(0, 2, 1)), in_hbm(w_out))
    w_all = lax.all_gather(w_own, "dp", axis=0, tiled=True)
    up, left, corner = edges(up, left, corner, 1)
    g_wire, masks, meta, x0, sel = pl.pallas_call(
        dispatch_g,
        out_shape=(
            bf16((n, WIDE)),
            bf16((3, n, tokens)),
            f32((tokens, tokens)),
            f32((tokens, width)),
            bf16((tokens, 4 * tc + 4 * tr + 16)),
        ),
        in_specs=[ANY] * 6,
        out_specs=(VMEM,) * 5,
        scratch_shapes=[
            pltpu.SMEM((2,), jnp.int32),
            pltpu.VMEM((2, tokens), jnp.int32),
            pltpu.VMEM((2, tokens), jnp.float32),
        ]
        + [pltpu.VMEM((tr, tc, width), jnp.bfloat16)] * 3
        + [pltpu.SemaphoreType.DMA((6,))],
        compiler_params=pltpu.CompilerParams(vmem_limit_bytes=32 * 1024 * 1024),
        cost_estimate=pl.CostEstimate(
            flops=4 * 256 * n * WIDE, bytes_accessed=1 << 20, transcendentals=0
        ),
    )(*(in_hbm(v) for v in (shift_offsets, ids, gates, d_out, attn_win, shortcut)))
    sent, x = call(
        dispatch_u,
        (bf16((n, 2 * WIDE)), f32((tokens, width))),
        g_wire, masks, x0, sel, up, left, corner,
        flops=4 * 128 * n * WIDE, traffic=1 << 21,
    )
    q_wire, y_wire, grads = experts(exchange(sent, n_ex), w_all)
    rq = exchange(q_wire, n_ex)
    ry = exchange(y_wire, n_ex)
    grad = lax.psum_scatter(grads, "dp", scatter_dimension=0, tiled=True)
    grad_in, grad_out = pl.pallas_call(
        widen,
        out_shape=(pltpu.HBM((1, part, width), jnp.float32),) * 2,
        in_specs=[ANY],
        out_specs=(ANY,) * 2,
        scratch_shapes=[
            pltpu.VMEM(grad.shape, jnp.bfloat16),
            pltpu.VMEM(grad.shape, jnp.float32),
            pltpu.SemaphoreType.DMA((4,)),
        ],
        compiler_params=pltpu.CompilerParams(vmem_limit_bytes=32 * 1024 * 1024),
        cost_estimate=pl.CostEstimate(flops=0, bytes_accessed=12 * part * width, transcendentals=0),
    )(in_hbm(grad))
    ds, ds_keep, up_b, left_b, corner_b = call(
        functools.partial(combine_q, tr, tc),
        (
            bf16((tokens, width)),
            bf16((tokens, width)),
            bf16((4 * tc, width)),
            bf16((4 * tr, width)),
            bf16((16, width)),
        ),
        rq, meta, x, dout,
        flops=1 << 40, traffic=1 << 21,
    )
    down, right, corner_r = edges(up_b, left_b, corner_b, -1)
    d_attn = call(
        functools.partial(roll_back, tr, tc),
        bf16((tokens, width)),
        shift_offsets, ds_keep, down, right, corner_r,
        specs=[SMEM] + [VMEM] * 4,
        flops=2 * tokens * 256 * width, traffic=1 << 19,
    )
    x, d_attn = lax.optimization_barrier((x, d_attn))
    block_out, d_gates = call(
        combine_y,
        (bf16((tokens, width)), f32((2, tokens))),
        ry, meta, x, dout,
        flops=8 * tokens * n * WIDE, traffic=1 << 21,
    )
    tile = (tr, tc, width)
    return (
        block_out.reshape(tile),
        ds.reshape(tile),
        d_attn.reshape(tile),
        d_gates.T.reshape(1, 1, tokens, 2),
        grad_in.transpose(0, 2, 1),
        grad_out,
    )


def solution(mesh):
    tile = P("dp", "expert", None)
    pairs = P("dp", "expert", None, None)
    first, second = P("expert", None, "dp"), P("expert", "dp", None)
    return jax.shard_map(
        per_device,
        mesh=mesh,
        in_specs=(tile, tile, tile, pairs, pairs, P(), first, second),
        out_specs=(tile, tile, tile, pairs, first, second),
        check_vma=False,
    )
```

```python
import functools

import jax
import jax.numpy as jnp
from jax import lax
from jax.experimental import pallas as pl
from jax.experimental.pallas import tpu as pltpu
from jax.sharding import PartitionSpec as P

CAP = 5
WIRE_ROWS = 8
WIDE = 512
EPS = 1e-05
VMEM = pl.BlockSpec(memory_space=pltpu.VMEM)
ANY = pl.BlockSpec(memory_space=pl.ANY)
SMEM = pl.BlockSpec(memory_space=pltpu.SMEM)


def iota(shape, dim):
    return lax.broadcasted_iota(jnp.int32, shape, dim)


def ones_where(mask):
    return jnp.where(mask, 1.0, 0.0).astype(jnp.bfloat16)


def dot(a, b):
    return jnp.dot(a, b, preferred_element_type=jnp.float32)


def dot_t(a, b):
    return lax.dot_general(a, b, (((1,), (1,)), ((), ())), preferred_element_type=jnp.float32)


def t_dot(a, b):
    return lax.dot_general(a, b, (((0,), (0,)), ((), ())), preferred_element_type=jnp.float32)


def in_hbm(x):
    return pltpu.with_memory_space_constraint(x, pltpu.HBM)


def call(body, outs, *args, flops=0, traffic=0, specs=None, **kw):
    return pl.pallas_call(
        body,
        out_shape=outs,
        in_specs=[VMEM] * len(args) if specs is None else specs,
        out_specs=jax.tree.map(lambda _: VMEM, outs),
        compiler_params=pltpu.CompilerParams(vmem_limit_bytes=32 * 1024 * 1024),
        cost_estimate=pl.CostEstimate(flops=flops, bytes_accessed=traffic, transcendentals=0),
        **kw,
    )(*args)


def wire_masks(row, shape, dim):
    at = iota(shape, dim)
    pos = row & 7
    tail = row - pos + CAP + (pos >> 1)
    odd = (pos & 1) == 1
    left = jnp.where(odd, -1, tail)
    right = jnp.where(odd, tail, -1)
    return ones_where(at == row), ones_where(at == left), ones_where(at == right)


def from_wire(masks, wire):
    head, left, right = masks
    half = WIDE // 2
    return (
        dot(head, wire),
        dot(left, wire[:, :half]) + dot(right, wire[:, half:]),
    )


def to_wire(masks, rows, turned):
    head, left, right = masks
    f = t_dot if turned else dot
    tail = rows[:, WIDE:]
    return f(head, rows[:, :WIDE]) + jnp.concatenate([f(left, tail), f(right, tail)], axis=1)


def prepare(attn_hbm, w1_hbm, w2_hbm, up_ref, left_ref, corner_ref, w_ref, attn_s, sems):
    copies = [
        pltpu.make_async_copy(src, dst, sems.at[i])
        for i, (src, dst) in enumerate(
            ((attn_hbm, attn_s), (w1_hbm, w_ref.at[:, 0]), (w2_hbm, w_ref.at[:, 1]))
        )
    ]
    for copy in copies:
        copy.start()
    tr, tc, width = attn_s.shape
    tokens = tr * tc
    n = 4 * tr
    s = iota((n, 1), 0)
    edge = ones_where((s // 4) * tc + tc - 4 + s % 4 == iota((n, tokens), 1))
    copies[0].wait()
    attn = attn_s[...].reshape(tokens, width)
    up_ref[...] = attn[tokens - 4 * tc :]
    left = dot(edge, attn).astype(jnp.bfloat16)
    left_ref[...] = left
    corner_ref[...] = left[n - 16 :]
    copies[1].wait()
    copies[2].wait()


def dispatch_g(
    off_hbm, ids_hbm, gates_hbm, dout_hbm, attn_hbm, short_hbm,
    sent_ref, mask_ref, meta_ref, x_ref, sel_ref,
    off_ref, ids_ref, gates_ref, dout_s, attn_s, short_s, sems,
):
    copies = [
        pltpu.make_async_copy(src, dst, sems.at[i])
        for i, (src, dst) in enumerate(
            (
                (off_hbm, off_ref),
                (ids_hbm, ids_ref),
                (gates_hbm, gates_ref),
                (attn_hbm, attn_s),
                (short_hbm, short_s),
                (dout_hbm, dout_s),
            )
        )
    ]
    for copy in copies:
        copy.start()
    for copy in copies:
        copy.wait()
    tr, tc, width = attn_s.shape
    tokens = tr * tc
    t = iota((tokens, 1), 0)
    inside, halo = places(t // tc - off_ref[0], t % tc - off_ref[1], tr, tc)
    sel_ref[...] = halo
    x_ref[...] = short_s[...].reshape(tokens, width).astype(jnp.float32) + dot(
        inside, attn_s[...].reshape(tokens, width)
    )
    n = sent_ref.shape[0]
    experts = n // WIRE_ROWS
    ids = ids_ref[...]
    rank = iota((experts, tokens), 0)
    first = jnp.where(ids[0:1] == rank, 1.0, 0.0)
    second = jnp.where(ids[1:2] == rank, 1.0, 0.0)
    earlier = ones_where(iota((tokens, tokens), 0) < iota((tokens, tokens), 1))
    before = dot((first + second).astype(jnp.bfloat16), earlier)
    row0 = ids[0:1] * WIRE_ROWS + jnp.sum(before * first, axis=0, keepdims=True).astype(jnp.int32)
    row1 = ids[1:2] * WIRE_ROWS + jnp.sum(before * second, axis=0, keepdims=True).astype(jnp.int32)
    at = iota((tokens, tokens), 0)
    table = jnp.where(at == 0, gates_ref[0:1], 0.0)
    table = jnp.where(at == 1, gates_ref[1:2], table)
    table = jnp.where(at == 2, row0.astype(jnp.float32), table)
    table = jnp.where(at == 3, row1.astype(jnp.float32), table)
    meta = table.T
    meta_ref[...] = meta
    dout = dout_s[...].reshape(tokens, width).astype(jnp.float32)
    sent = 0.0
    both = None
    for k, row in enumerate((row0, row1)):
        masks = wire_masks(row, (n, tokens), 0)
        sent = sent + to_wire(masks, (meta[:, k : k + 1] * dout).astype(jnp.bfloat16), False)
        both = masks if both is None else tuple(a + b for a, b in zip(both, masks))
    for m in range(3):
        mask_ref[m] = both[m]
    sent_ref[...] = sent.astype(jnp.bfloat16)


def normalize(x):
    m = jnp.mean(x, axis=-1, keepdims=True)
    c = x - m
    r = lax.rsqrt(jnp.mean(c * c, axis=-1, keepdims=True) + EPS)
    return c * r, r


def places(i, j, tr, tc):
    tokens = i.shape[0]
    i_in = (i >= 0) & (i < tr)
    j_in = (j >= 0) & (j < tc)
    ei = jnp.where(i < 0, i + 4, i - tr)
    ej = jnp.where(j < 0, j + 4, j - tc)
    own = jnp.where(i_in & j_in, i * tc + j, -1)
    edge = jnp.where(
        i_in,
        jnp.where(j_in, -1, 4 * tc + i * 4 + ej),
        jnp.where(j_in, ei * tc + j, 4 * tc + 4 * tr + ei * 4 + ej),
    )
    count = 4 * tc + 4 * tr + 16
    return (
        ones_where(own == iota((tokens, tokens), 1)),
        ones_where(edge == iota((tokens, count), 1)),
    )


def dispatch_u(g_ref, mask_ref, x0_ref, sel_ref, up_ref, left_ref, corner_ref, sent_ref, x_ref):
    edge = jnp.concatenate([up_ref[...], left_ref[...], corner_ref[...]], axis=0)
    x = x0_ref[...] + dot(sel_ref[...], edge)
    x_ref[...] = x
    xhat, _ = normalize(x)
    masks = tuple(mask_ref[m] for m in range(3))
    sent_ref[:, :WIDE] = g_ref[...]
    sent_ref[:, WIDE:] = to_wire(masks, xhat.astype(jnp.bfloat16), False).astype(jnp.bfloat16)


def slot_masks(dim, peers):
    slots = peers * CAP
    s = iota((slots, 1) if dim else (1, slots), 1 - dim)
    row = (s % peers) * WIRE_ROWS + s // peers
    wire = peers * WIRE_ROWS
    return wire_masks(row, (slots, wire) if dim else (wire, slots), dim)


def send_slots(rows_of, out_ref, at):
    n = out_ref.shape[0]
    peers = min(32, n // WIRE_ROWS)
    rows, slots = peers * WIRE_ROWS, peers * CAP
    masks = slot_masks(0, peers)
    for b in range(n // rows):
        block = to_wire(masks, rows_of[b * slots : (b + 1) * slots], False)
        out_ref[b * rows : (b + 1) * rows, at : at + WIDE] = block.astype(jnp.bfloat16)


def experts_body(wire_ref, w_hbm, out_ref, grad_hbm, w_s, grad_s, u_s, g_s, in_sems, out_sems):
    parts, _, part, width = w_s.shape
    half = parts // 2
    hidden = half * part
    pieces = [(c, k) for c in range(2) for k in range(2)]
    ins = [
        pltpu.make_async_copy(
            w_hbm.at[pl.ds(c * half, half), k], w_s.at[pl.ds(c * half, half), k], in_sems.at[i]
        )
        for i, (c, k) in enumerate(pieces)
    ]
    outs = [
        pltpu.make_async_copy(
            grad_s.at[pl.ds(c * half, half), k], grad_hbm.at[pl.ds(c * half, half), k], out_sems.at[i]
        )
        for i, (c, k) in enumerate(pieces)
    ]
    for copy in ins:
        copy.start()
    n = wire_ref.shape[0]
    peers = min(32, n // WIRE_ROWS)
    rows, slots = peers * WIRE_ROWS, peers * CAP
    masks = slot_masks(1, peers)
    for b in range(n // rows):
        for at, dst in ((0, g_s), (WIDE, u_s)):
            head, tail = from_wire(masks, wire_ref[b * rows : (b + 1) * rows, at : at + WIDE])
            dst[b * slots : (b + 1) * slots, :WIDE] = head.astype(jnp.bfloat16)
            dst[b * slots : (b + 1) * slots, WIDE:] = tail.astype(jnp.bfloat16)
    u = u_s[...]
    g = g_s[...]

    def weights(c, k):
        return w_s[c * half : (c + 1) * half, k].reshape(hidden, width)

    pairs = []
    for c in range(2):
        ins[2 * c].wait()
        h = dot_t(u, weights(c, 0))
        ins[2 * c + 1].wait()
        pairs.append((h, dot_t(g, weights(c, 1))))
    acts = []
    for c, (h, da) in enumerate(pairs):
        cdf = 0.5 * (1.0 + lax.erf(h * 0.7071067811865476))
        pdf = jnp.exp(-0.5 * h * h) * 0.3989422804014327
        a = (h * cdf).astype(jnp.bfloat16)
        p = (da * (cdf + h * pdf)).astype(jnp.bfloat16)
        acts.append((p, a))
        for k, (left, right) in enumerate(((p, u), (a, g))):
            grad = t_dot(left, right).astype(jnp.bfloat16)
            grad_s[c * half : (c + 1) * half, k] = grad.reshape(half, part, width)
            outs[2 * c + k].start()
    q = dot(acts[0][0], weights(0, 0)) + dot(acts[1][0], weights(1, 0))
    y = dot(acts[0][1], weights(0, 1)) + dot(acts[1][1], weights(1, 1))
    send_slots(q.astype(jnp.bfloat16), out_ref, 0)
    send_slots(y.astype(jnp.bfloat16), out_ref, WIDE)
    for copy in outs:
        copy.wait()


def experts(wire, w):
    n = wire.shape[0]
    parts, _, part, width = w.shape
    slots = n // WIRE_ROWS * CAP
    hidden = parts * part
    return pl.pallas_call(
        experts_body,
        out_shape=(
            jax.ShapeDtypeStruct((n, 2 * WIDE), jnp.bfloat16),
            pltpu.HBM(w.shape, jnp.bfloat16),
        ),
        in_specs=[VMEM, ANY],
        out_specs=(VMEM, ANY),
        scratch_shapes=[
            pltpu.VMEM(w.shape, jnp.bfloat16),
            pltpu.VMEM(w.shape, jnp.bfloat16),
            pltpu.VMEM((slots, width), jnp.bfloat16),
            pltpu.VMEM((slots, width), jnp.bfloat16),
            pltpu.SemaphoreType.DMA((4,)),
            pltpu.SemaphoreType.DMA((4,)),
        ],
        compiler_params=pltpu.CompilerParams(vmem_limit_bytes=40 << 20),
        cost_estimate=pl.CostEstimate(
            flops=12 * slots * hidden * width,
            bytes_accessed=8 * hidden * width,
            transcendentals=2 * slots * hidden,
        ),
    )(wire, in_hbm(w))


def combine_q(tr, tc, wire_ref, meta_ref, x_ref, dout_ref, ds_ref, keep_ref, up_ref, left_ref, corner_ref):
    wire = wire_ref[:, :WIDE]
    tokens = x_ref.shape[0]
    both = None
    for k in range(2):
        row = meta_ref[:, 2 + k : 3 + k].astype(jnp.int32)
        masks = wire_masks(row, (tokens, wire.shape[0]), 1)
        both = masks if both is None else tuple(a + b for a, b in zip(both, masks))
    du = jnp.concatenate(from_wire(both, wire), axis=1)
    xhat, r = normalize(x_ref[...])
    dx = r * (
        du
        - jnp.mean(du, axis=-1, keepdims=True)
        - xhat * jnp.mean(du * xhat, axis=-1, keepdims=True)
    )
    ds = (dout_ref[...].astype(jnp.float32) + dx).astype(jnp.bfloat16)
    ds_ref[...] = ds
    keep_ref[...] = ds
    up_ref[...] = ds[: 4 * tc]
    n = 4 * tr
    s = iota((n, 1), 0)
    edge = dot(ones_where((s // 4) * tc + s % 4 == iota((n, tokens), 1)), ds).astype(jnp.bfloat16)
    left_ref[...] = edge
    corner_ref[...] = edge[:16]


def roll_back(tr, tc, off_ref, ds_ref, down_ref, right_ref, corner_ref, out_ref):
    t = iota((ds_ref.shape[0], 1), 0)
    inside, halo = places(t // tc + off_ref[0], t % tc + off_ref[1], tr, tc)
    edge = jnp.concatenate([down_ref[...], right_ref[...], corner_ref[...]], axis=0)
    out_ref[...] = (dot(inside, ds_ref[...]) + dot(halo, edge)).astype(jnp.bfloat16)


def combine_y(
    wire_ref, meta_ref, x_ref, dout_ref, grad_hbm, out_ref, dg_ref, first_hbm, second_hbm,
    grad_s, wide_s, sems,
):
    wides = (first_hbm, second_hbm)
    fetch = [pltpu.make_async_copy(grad_hbm.at[:, k], grad_s.at[:, k], sems.at[k]) for k in range(2)]
    store = [pltpu.make_async_copy(wide_s.at[:, k], wides[k], sems.at[2 + k]) for k in range(2)]
    for copy in fetch:
        copy.start()
    wire = wire_ref[:, WIDE:]
    dout = dout_ref[...].astype(jnp.float32)
    tokens = dout.shape[0]
    masks = [
        wire_masks(meta_ref[:, 2 + k : 3 + k].astype(jnp.int32), (tokens, wire.shape[0]), 1)
        for k in range(2)
    ]
    ys = [jnp.concatenate(from_wire(m, wire), axis=1) for m in masks]
    for k in range(2):
        fetch[k].wait()
        wide_s[:, k] = grad_s[:, k].astype(jnp.float32)
        store[k].start()
    total = x_ref[...]
    lane = iota((tokens, tokens), 1)
    table = jnp.zeros((tokens, tokens), jnp.float32)
    for k, y in enumerate(ys):
        total = total + meta_ref[:, k : k + 1] * y
        table = jnp.where(lane == k, jnp.sum(dout * y, axis=-1, keepdims=True), table)
    out_ref[...] = total.astype(jnp.bfloat16)
    dg_ref[...] = table.T[:2]
    for copy in store:
        copy.wait()


def exchange(wire, n):
    blocks = wire.reshape(n, WIRE_ROWS, wire.shape[-1])
    out = lax.all_to_all(blocks, "expert", split_axis=0, concat_axis=0, tiled=True)
    return out.reshape(wire.shape)


def edges(row_edge, col_edge, corner, step):
    n_dp, n_ex = lax.axis_size("dp"), lax.axis_size("expert")
    by_dp = [(i, (i + step) % n_dp) for i in range(n_dp)]
    by_ex = [(i, (i + step) % n_ex) for i in range(n_ex)]
    by_both = [
        (q * n_dp + p, (q + step) % n_ex * n_dp + (p + step) % n_dp)
        for q in range(n_ex)
        for p in range(n_dp)
    ]
    return (
        lax.ppermute(row_edge, "dp", by_dp),
        lax.ppermute(col_edge, "expert", by_ex),
        lax.ppermute(corner, ("expert", "dp"), by_both),
    )


def per_device(attn_win, shortcut, d_out, expert_ids, gate_probs, shift_offsets, w_in, w_out):
    tr, tc, width = attn_win.shape
    tokens = tr * tc
    n_ex = lax.axis_size("expert")
    n = n_ex * WIRE_ROWS
    bf16 = functools.partial(jax.ShapeDtypeStruct, dtype=jnp.bfloat16)
    f32 = functools.partial(jax.ShapeDtypeStruct, dtype=jnp.float32)
    ids = expert_ids.reshape(tokens, 2).T
    gates = gate_probs.reshape(tokens, 2).T
    dout = d_out.reshape(tokens, width)
    part = w_out.shape[1]

    up, left, corner, w_own = pl.pallas_call(
        prepare,
        out_shape=(
            bf16((4 * tc, width)),
            bf16((4 * tr, width)),
            bf16((16, width)),
            bf16((1, 2, part, width)),
        ),
        in_specs=[ANY] * 3,
        out_specs=(VMEM,) * 4,
        scratch_shapes=[pltpu.VMEM((tr, tc, width), jnp.bfloat16), pltpu.SemaphoreType.DMA((3,))],
        compiler_params=pltpu.CompilerParams(vmem_limit_bytes=32 * 1024 * 1024),
        cost_estimate=pl.CostEstimate(flops=1 << 25, bytes_accessed=1 << 21, transcendentals=0),
    )(in_hbm(attn_win), in_hbm(w_in.transpose(0, 2, 1)), in_hbm(w_out))
    w_all = lax.all_gather(w_own, "dp", axis=0, tiled=True)
    up, left, corner = edges(up, left, corner, 1)
    g_wire, masks, meta, x0, sel = pl.pallas_call(
        dispatch_g,
        out_shape=(
            bf16((n, WIDE)),
            bf16((3, n, tokens)),
            f32((tokens, tokens)),
            f32((tokens, width)),
            bf16((tokens, 4 * tc + 4 * tr + 16)),
        ),
        in_specs=[ANY] * 6,
        out_specs=(VMEM,) * 5,
        scratch_shapes=[
            pltpu.SMEM((2,), jnp.int32),
            pltpu.VMEM((2, tokens), jnp.int32),
            pltpu.VMEM((2, tokens), jnp.float32),
        ]
        + [pltpu.VMEM((tr, tc, width), jnp.bfloat16)] * 3
        + [pltpu.SemaphoreType.DMA((6,))],
        compiler_params=pltpu.CompilerParams(vmem_limit_bytes=32 * 1024 * 1024),
        cost_estimate=pl.CostEstimate(
            flops=4 * 256 * n * WIDE, bytes_accessed=1 << 20, transcendentals=0
        ),
    )(*(in_hbm(v) for v in (shift_offsets, ids, gates, d_out, attn_win, shortcut)))
    sent, x = call(
        dispatch_u,
        (bf16((n, 2 * WIDE)), f32((tokens, width))),
        g_wire, masks, x0, sel, up, left, corner,
        flops=4 * 128 * n * WIDE, traffic=1 << 21,
    )
    returned, grads = experts(exchange(sent, n_ex), w_all)
    returned = exchange(returned, n_ex)
    grad = lax.psum_scatter(grads, "dp", scatter_dimension=0, tiled=True)
    ds, ds_keep, up_b, left_b, corner_b = call(
        functools.partial(combine_q, tr, tc),
        (
            bf16((tokens, width)),
            bf16((tokens, width)),
            bf16((4 * tc, width)),
            bf16((4 * tr, width)),
            bf16((16, width)),
        ),
        returned, meta, x, dout,
        flops=4 * tokens * n * WIDE, traffic=1 << 21,
    )
    down, right, corner_r = edges(up_b, left_b, corner_b, -1)
    block_out, d_gates, grad_in, grad_out = pl.pallas_call(
        combine_y,
        out_shape=(bf16((tokens, width)), f32((2, tokens)))
        + (pltpu.HBM((1, part, width), jnp.float32),) * 2,
        in_specs=[VMEM] * 4 + [ANY],
        out_specs=(VMEM, VMEM, ANY, ANY),
        scratch_shapes=[
            pltpu.VMEM(grad.shape, jnp.bfloat16),
            pltpu.VMEM(grad.shape, jnp.float32),
            pltpu.SemaphoreType.DMA((4,)),
        ],
        compiler_params=pltpu.CompilerParams(vmem_limit_bytes=32 * 1024 * 1024),
        cost_estimate=pl.CostEstimate(
            flops=8 * tokens * n * WIDE, bytes_accessed=1 << 21, transcendentals=0
        ),
    )(returned, meta, x, dout, in_hbm(grad))
    ds_keep, block_out = lax.optimization_barrier((ds_keep, block_out))
    d_attn = call(
        functools.partial(roll_back, tr, tc),
        bf16((tokens, width)),
        shift_offsets, ds_keep, down, right, corner_r,
        specs=[SMEM] + [VMEM] * 4,
        flops=2 * tokens * 256 * width, traffic=1 << 19,
    )
    tile = (tr, tc, width)
    return (
        block_out.reshape(tile),
        ds.reshape(tile),
        d_attn.reshape(tile),
        d_gates.T.reshape(1, 1, tokens, 2),
        grad_in.transpose(0, 2, 1),
        grad_out,
    )


def solution(mesh):
    tile = P("dp", "expert", None)
    pairs = P("dp", "expert", None, None)
    first, second = P("expert", None, "dp"), P("expert", "dp", None)
    return jax.shard_map(
        per_device,
        mesh=mesh,
        in_specs=(tile, tile, tile, pairs, pairs, P(), first, second),
        out_specs=(tile, tile, tile, pairs, first, second),
        check_vma=False,
    )
```

```python
import functools

import jax
import jax.numpy as jnp
from jax import lax
from jax.experimental import pallas as pl
from jax.experimental.pallas import tpu as pltpu
from jax.sharding import PartitionSpec as P

CAP = 5
WIRE_ROWS = 8
WIDE = 512
EPS = 1e-05
VMEM = pl.BlockSpec(memory_space=pltpu.VMEM)
ANY = pl.BlockSpec(memory_space=pl.ANY)
SMEM = pl.BlockSpec(memory_space=pltpu.SMEM)


def iota(shape, dim):
    return lax.broadcasted_iota(jnp.int32, shape, dim)


def ones_where(mask):
    return jnp.where(mask, 1.0, 0.0).astype(jnp.bfloat16)


def dot(a, b):
    return jnp.dot(a, b, preferred_element_type=jnp.float32)


def dot_t(a, b):
    return lax.dot_general(a, b, (((1,), (1,)), ((), ())), preferred_element_type=jnp.float32)


def t_dot(a, b):
    return lax.dot_general(a, b, (((0,), (0,)), ((), ())), preferred_element_type=jnp.float32)


def in_hbm(x):
    return pltpu.with_memory_space_constraint(x, pltpu.HBM)


def call(body, outs, *args, flops=0, traffic=0, specs=None, **kw):
    return pl.pallas_call(
        body,
        out_shape=outs,
        in_specs=[VMEM] * len(args) if specs is None else specs,
        out_specs=jax.tree.map(lambda _: VMEM, outs),
        compiler_params=pltpu.CompilerParams(vmem_limit_bytes=32 * 1024 * 1024),
        cost_estimate=pl.CostEstimate(flops=flops, bytes_accessed=traffic, transcendentals=0),
        **kw,
    )(*args)


def wire_masks(row, shape, dim):
    at = iota(shape, dim)
    pos = row & 7
    tail = row - pos + CAP + (pos >> 1)
    odd = (pos & 1) == 1
    left = jnp.where(odd, -1, tail)
    right = jnp.where(odd, tail, -1)
    return ones_where(at == row), ones_where(at == left), ones_where(at == right)


def from_wire(masks, wire):
    head, left, right = masks
    half = WIDE // 2
    return (
        dot(head, wire),
        dot(left, wire[:, :half]) + dot(right, wire[:, half:]),
    )


def to_wire(masks, rows, turned):
    head, left, right = masks
    f = t_dot if turned else dot
    tail = rows[:, WIDE:]
    return f(head, rows[:, :WIDE]) + jnp.concatenate([f(left, tail), f(right, tail)], axis=1)


def prepare(attn_hbm, up_ref, left_ref, corner_ref, attn_s, sem):
    copy = pltpu.make_async_copy(attn_hbm, attn_s, sem)
    copy.start()
    tr, tc, width = attn_s.shape
    tokens = tr * tc
    n = 4 * tr
    s = iota((n, 1), 0)
    edge = ones_where((s // 4) * tc + tc - 4 + s % 4 == iota((n, tokens), 1))
    copy.wait()
    attn = attn_s[...].reshape(tokens, width)
    up_ref[...] = attn[tokens - 4 * tc :]
    left = dot(edge, attn).astype(jnp.bfloat16)
    left_ref[...] = left
    corner_ref[...] = left[n - 16 :]


def dispatch_g(
    off_hbm, ids_hbm, gates_hbm, dout_hbm, attn_hbm, short_hbm, w1_hbm, w2_hbm,
    sent_ref, mask_ref, meta_ref, x_ref, sel_ref, w_ref,
    off_ref, ids_ref, gates_ref, dout_s, attn_s, short_s, sems,
):
    copies = [
        pltpu.make_async_copy(src, dst, sems.at[i])
        for i, (src, dst) in enumerate(
            (
                (off_hbm, off_ref),
                (ids_hbm, ids_ref),
                (gates_hbm, gates_ref),
                (attn_hbm, attn_s),
                (short_hbm, short_s),
                (dout_hbm, dout_s),
                (w1_hbm, w_ref.at[0:1]),
                (w2_hbm, w_ref.at[1:2]),
            )
        )
    ]
    for copy in copies:
        copy.start()
    for copy in copies[:6]:
        copy.wait()
    tr, tc, width = attn_s.shape
    tokens = tr * tc
    t = iota((tokens, 1), 0)
    inside, halo = places(t // tc - off_ref[0], t % tc - off_ref[1], tr, tc)
    sel_ref[...] = halo
    x_ref[...] = short_s[...].reshape(tokens, width).astype(jnp.float32) + dot(
        inside, attn_s[...].reshape(tokens, width)
    )
    n = sent_ref.shape[0]
    experts = n // WIRE_ROWS
    ids = ids_ref[...]
    rank = iota((experts, tokens), 0)
    first = jnp.where(ids[0:1] == rank, 1.0, 0.0)
    second = jnp.where(ids[1:2] == rank, 1.0, 0.0)
    earlier = ones_where(iota((tokens, tokens), 0) < iota((tokens, tokens), 1))
    before = dot((first + second).astype(jnp.bfloat16), earlier)
    row0 = ids[0:1] * WIRE_ROWS + jnp.sum(before * first, axis=0, keepdims=True).astype(jnp.int32)
    row1 = ids[1:2] * WIRE_ROWS + jnp.sum(before * second, axis=0, keepdims=True).astype(jnp.int32)
    at = iota((tokens, tokens), 0)
    table = jnp.where(at == 0, gates_ref[0:1], 0.0)
    table = jnp.where(at == 1, gates_ref[1:2], table)
    table = jnp.where(at == 2, row0.astype(jnp.float32), table)
    table = jnp.where(at == 3, row1.astype(jnp.float32), table)
    meta = table.T
    meta_ref[...] = meta
    dout = dout_s[...].reshape(tokens, width).astype(jnp.float32)
    sent = 0.0
    both = None
    for k, row in enumerate((row0, row1)):
        masks = wire_masks(row, (n, tokens), 0)
        sent = sent + to_wire(masks, (meta[:, k : k + 1] * dout).astype(jnp.bfloat16), False)
        both = masks if both is None else tuple(a + b for a, b in zip(both, masks))
    for m in range(3):
        mask_ref[m] = both[m]
    sent_ref[...] = sent.astype(jnp.bfloat16)
    for copy in copies[6:]:
        copy.wait()


def normalize(x):
    m = jnp.mean(x, axis=-1, keepdims=True)
    c = x - m
    r = lax.rsqrt(jnp.mean(c * c, axis=-1, keepdims=True) + EPS)
    return c * r, r


def places(i, j, tr, tc):
    tokens = i.shape[0]
    i_in = (i >= 0) & (i < tr)
    j_in = (j >= 0) & (j < tc)
    ei = jnp.where(i < 0, i + 4, i - tr)
    ej = jnp.where(j < 0, j + 4, j - tc)
    own = jnp.where(i_in & j_in, i * tc + j, -1)
    edge = jnp.where(
        i_in,
        jnp.where(j_in, -1, 4 * tc + i * 4 + ej),
        jnp.where(j_in, ei * tc + j, 4 * tc + 4 * tr + ei * 4 + ej),
    )
    count = 4 * tc + 4 * tr + 16
    return (
        ones_where(own == iota((tokens, tokens), 1)),
        ones_where(edge == iota((tokens, count), 1)),
    )


def dispatch_u(g_ref, mask_ref, x0_ref, sel_ref, up_ref, left_ref, corner_ref, sent_ref, x_ref):
    edge = jnp.concatenate([up_ref[...], left_ref[...], corner_ref[...]], axis=0)
    x = x0_ref[...] + dot(sel_ref[...], edge)
    x_ref[...] = x
    xhat, _ = normalize(x)
    masks = tuple(mask_ref[m] for m in range(3))
    sent_ref[:, :WIDE] = g_ref[...]
    sent_ref[:, WIDE:] = to_wire(masks, xhat.astype(jnp.bfloat16), False).astype(jnp.bfloat16)


def slot_masks(dim, peers):
    slots = peers * CAP
    s = iota((slots, 1) if dim else (1, slots), 1 - dim)
    row = (s % peers) * WIRE_ROWS + s // peers
    wire = peers * WIRE_ROWS
    return wire_masks(row, (slots, wire) if dim else (wire, slots), dim)


def send_slots(rows_of, out_ref, at):
    n = out_ref.shape[0]
    peers = min(32, n // WIRE_ROWS)
    rows, slots = peers * WIRE_ROWS, peers * CAP
    masks = slot_masks(0, peers)
    for b in range(n // rows):
        block = to_wire(masks, rows_of[b * slots : (b + 1) * slots], False)
        out_ref[b * rows : (b + 1) * rows, at : at + WIDE] = block.astype(jnp.bfloat16)


def experts_body(wire_ref, *refs):
    half = (len(refs) - 9) // 2
    pieces_hbm = refs[: 2 * half]
    out_ref, *grads_hbm, w_s, grad_s, u_s, g_s, in_sems, out_sems = refs[2 * half :]
    _, _, part, width = w_s.shape
    hidden = half * part
    ins = [
        pltpu.make_async_copy(piece, w_s.at[i], in_sems.at[i]) for i, piece in enumerate(pieces_hbm)
    ]
    outs = [
        pltpu.make_async_copy(
            grad_s.at[pl.ds(c * half, half), k], grads_hbm[c].at[:, k], out_sems.at[2 * c + k]
        )
        for c in range(2)
        for k in range(2)
    ]
    for copy in ins:
        copy.start()
    n = wire_ref.shape[0]
    peers = min(32, n // WIRE_ROWS)
    rows, slots = peers * WIRE_ROWS, peers * CAP
    masks = slot_masks(1, peers)
    for b in range(n // rows):
        for at, dst in ((0, g_s), (WIDE, u_s)):
            head, tail = from_wire(masks, wire_ref[b * rows : (b + 1) * rows, at : at + WIDE])
            dst[b * slots : (b + 1) * slots, :WIDE] = head.astype(jnp.bfloat16)
            dst[b * slots : (b + 1) * slots, WIDE:] = tail.astype(jnp.bfloat16)
    u = u_s[...]
    g = g_s[...]

    def weights(c, k):
        return w_s[c * half : (c + 1) * half, k].reshape(hidden, width)

    pairs = []
    for c in range(2):
        for copy in ins[c * half : (c + 1) * half]:
            copy.wait()
        h = dot_t(u, weights(c, 0))
        pairs.append((h, dot_t(g, weights(c, 1))))
    acts = []
    for c, (h, da) in enumerate(pairs):
        cdf = 0.5 * (1.0 + lax.erf(h * 0.7071067811865476))
        pdf = jnp.exp(-0.5 * h * h) * 0.3989422804014327
        a = (h * cdf).astype(jnp.bfloat16)
        p = (da * (cdf + h * pdf)).astype(jnp.bfloat16)
        acts.append((p, a))
        for k, (left, right) in enumerate(((p, u), (a, g))):
            grad = t_dot(left, right).astype(jnp.bfloat16)
            grad_s[c * half : (c + 1) * half, k] = grad.reshape(half, part, width)
            outs[2 * c + k].start()
    q = dot(acts[0][0], weights(0, 0)) + dot(acts[1][0], weights(1, 0))
    y = dot(acts[0][1], weights(0, 1)) + dot(acts[1][1], weights(1, 1))
    send_slots(q.astype(jnp.bfloat16), out_ref, 0)
    send_slots(y.astype(jnp.bfloat16), out_ref, WIDE)
    for copy in outs:
        copy.wait()


def experts(wire, mine, theirs):
    n = wire.shape[0]
    _, part, width = mine[0].shape
    half = len(mine)
    slots = n // WIRE_ROWS * CAP
    hidden = 2 * half * part
    return pl.pallas_call(
        experts_body,
        out_shape=(jax.ShapeDtypeStruct((n, 2 * WIDE), jnp.bfloat16),)
        + (pltpu.HBM((half, 2, part, width), jnp.bfloat16),) * 2,
        in_specs=[VMEM] + [ANY] * (2 * half),
        out_specs=(VMEM, ANY, ANY),
        scratch_shapes=[
            pltpu.VMEM((2 * half, 2, part, width), jnp.bfloat16),
            pltpu.VMEM((2 * half, 2, part, width), jnp.bfloat16),
            pltpu.VMEM((slots, width), jnp.bfloat16),
            pltpu.VMEM((slots, width), jnp.bfloat16),
            pltpu.SemaphoreType.DMA((2 * half,)),
            pltpu.SemaphoreType.DMA((4,)),
        ],
        compiler_params=pltpu.CompilerParams(vmem_limit_bytes=40 << 20),
        cost_estimate=pl.CostEstimate(
            flops=12 * slots * hidden * width,
            bytes_accessed=8 * hidden * width,
            transcendentals=2 * slots * hidden,
        ),
    )(wire, *(in_hbm(v) for v in (*mine, *theirs)))


def relay_body(*refs):
    n = len(refs) // 2
    sems = refs[-1]
    copies = [
        pltpu.make_async_copy(src, dst, sems.at[i])
        for i, (src, dst) in enumerate(zip(refs[:n], refs[n : 2 * n]))
    ]
    for copy in copies:
        copy.start()
    for copy in copies:
        copy.wait()


def relay(pieces):
    return pl.pallas_call(
        relay_body,
        out_shape=tuple(pltpu.HBM(v.shape, v.dtype) for v in pieces),
        in_specs=[VMEM] * len(pieces),
        out_specs=(ANY,) * len(pieces),
        scratch_shapes=[pltpu.SemaphoreType.DMA((len(pieces),))],
        compiler_params=pltpu.CompilerParams(vmem_limit_bytes=24 << 20),
        cost_estimate=pl.CostEstimate(flops=12 << 30, bytes_accessed=1 << 22, transcendentals=0),
    )(*pieces)


def pair_sum_body(mine_hbm, swapped_hbm, *refs):
    half = mine_hbm.shape[0]
    outs = refs[:half]
    a_s, b_s, kept_s, sum_s, in_sems, out_sems = refs[half:]
    ins = [
        pltpu.make_async_copy(src.at[d], dst.at[d], in_sems.at[2 * d + k])
        for d in range(half)
        for k, (src, dst) in enumerate(((mine_hbm, a_s), (swapped_hbm, b_s)))
    ]
    stores = [pltpu.make_async_copy(kept_s, outs[0], out_sems.at[0])] + [
        pltpu.make_async_copy(sum_s.at[d], outs[d], out_sems.at[d]) for d in range(1, half)
    ]
    for copy in ins:
        copy.start()
    for d in (*range(1, half), 0):
        ins[2 * d].wait()
        ins[2 * d + 1].wait()
        total = a_s[d].astype(jnp.float32) + b_s[d].astype(jnp.float32)
        if d == 0:
            kept_s[...] = total
        else:
            sum_s[d] = total.astype(jnp.bfloat16)
        stores[d].start()
    for copy in stores:
        copy.wait()


def pair_sum(mine, swapped):
    half, *rest = mine.shape
    return pl.pallas_call(
        pair_sum_body,
        out_shape=(pltpu.HBM(tuple(rest), jnp.float32),)
        + (pltpu.HBM(tuple(rest), jnp.bfloat16),) * (half - 1),
        in_specs=[ANY] * 2,
        out_specs=(ANY,) * half,
        scratch_shapes=[pltpu.VMEM(mine.shape, jnp.bfloat16)] * 2
        + [pltpu.VMEM(tuple(rest), jnp.float32), pltpu.VMEM(mine.shape, jnp.bfloat16)]
        + [pltpu.SemaphoreType.DMA((2 * half,)), pltpu.SemaphoreType.DMA((half,))],
        compiler_params=pltpu.CompilerParams(vmem_limit_bytes=40 << 20),
        cost_estimate=pl.CostEstimate(flops=0, bytes_accessed=8 * mine.size, transcendentals=0),
    )(in_hbm(mine), in_hbm(swapped))


def combine_q(tr, tc, wire_ref, meta_ref, x_ref, dout_ref, ds_ref, keep_ref, up_ref, left_ref, corner_ref):
    wire = wire_ref[:, :WIDE]
    tokens = x_ref.shape[0]
    both = None
    for k in range(2):
        row = meta_ref[:, 2 + k : 3 + k].astype(jnp.int32)
        masks = wire_masks(row, (tokens, wire.shape[0]), 1)
        both = masks if both is None else tuple(a + b for a, b in zip(both, masks))
    du = jnp.concatenate(from_wire(both, wire), axis=1)
    xhat, r = normalize(x_ref[...])
    dx = r * (
        du
        - jnp.mean(du, axis=-1, keepdims=True)
        - xhat * jnp.mean(du * xhat, axis=-1, keepdims=True)
    )
    ds = (dout_ref[...].astype(jnp.float32) + dx).astype(jnp.bfloat16)
    ds_ref[...] = ds
    keep_ref[...] = ds
    up_ref[...] = ds[: 4 * tc]
    n = 4 * tr
    s = iota((n, 1), 0)
    edge = dot(ones_where((s // 4) * tc + s % 4 == iota((n, tokens), 1)), ds).astype(jnp.bfloat16)
    left_ref[...] = edge
    corner_ref[...] = edge[:16]


def roll_back(tr, tc, off_ref, ds_ref, down_ref, right_ref, corner_ref, out_ref):
    t = iota((ds_ref.shape[0], 1), 0)
    inside, halo = places(t // tc + off_ref[0], t % tc + off_ref[1], tr, tc)
    edge = jnp.concatenate([down_ref[...], right_ref[...], corner_ref[...]], axis=0)
    out_ref[...] = (dot(inside, ds_ref[...]) + dot(halo, edge)).astype(jnp.bfloat16)


def combine_y(wire_ref, meta_ref, x_ref, dout_ref, kept_hbm, *refs):
    *others, out_ref, dg_ref, first_hbm, second_hbm, kept_s, wide_s, sems = refs
    wides = (first_hbm, second_hbm)
    fetch = pltpu.make_async_copy(kept_hbm, kept_s, sems.at[0])
    store = [pltpu.make_async_copy(wide_s.at[k : k + 1], wides[k], sems.at[1 + k]) for k in range(2)]
    fetch.start()
    wire = wire_ref[:, WIDE:]
    dout = dout_ref[...].astype(jnp.float32)
    tokens = dout.shape[0]
    masks = [
        wire_masks(meta_ref[:, 2 + k : 3 + k].astype(jnp.int32), (tokens, wire.shape[0]), 1)
        for k in range(2)
    ]
    ys = [jnp.concatenate(from_wire(m, wire), axis=1) for m in masks]
    fetch.wait()
    for k in range(2):
        grad = kept_s[k]
        for other in others:
            grad = grad + other[k].astype(jnp.float32)
        wide_s[k] = grad
        store[k].start()
    total = x_ref[...]
    lane = iota((tokens, tokens), 1)
    table = jnp.zeros((tokens, tokens), jnp.float32)
    for k, y in enumerate(ys):
        total = total + meta_ref[:, k : k + 1] * y
        table = jnp.where(lane == k, jnp.sum(dout * y, axis=-1, keepdims=True), table)
    out_ref[...] = total.astype(jnp.bfloat16)
    dg_ref[...] = table.T[:2]
    for copy in store:
        copy.wait()


def other_core(v):
    return lax.ppermute(v, "dp", [(i, i ^ 1) for i in range(lax.axis_size("dp"))])


def along_x(v, d):
    n = lax.axis_size("dp")
    return lax.ppermute(v, "dp", [(i, (i + 2 * d) % n) for i in range(n)])


def exchange(wire, n):
    blocks = wire.reshape(n, WIRE_ROWS, wire.shape[-1])
    out = lax.all_to_all(blocks, "expert", split_axis=0, concat_axis=0, tiled=True)
    return out.reshape(wire.shape)


def edges(row_edge, col_edge, corner, step):
    n_dp, n_ex = lax.axis_size("dp"), lax.axis_size("expert")
    by_dp = [(i, (i + step) % n_dp) for i in range(n_dp)]
    by_ex = [(i, (i + step) % n_ex) for i in range(n_ex)]
    by_both = [
        (q * n_dp + p, (q + step) % n_ex * n_dp + (p + step) % n_dp)
        for q in range(n_ex)
        for p in range(n_dp)
    ]
    return (
        lax.ppermute(row_edge, "dp", by_dp),
        lax.ppermute(col_edge, "expert", by_ex),
        lax.ppermute(corner, ("expert", "dp"), by_both),
    )


def per_device(attn_win, shortcut, d_out, expert_ids, gate_probs, shift_offsets, w_in, w_out):
    tr, tc, width = attn_win.shape
    tokens = tr * tc
    n_ex = lax.axis_size("expert")
    n = n_ex * WIRE_ROWS
    bf16 = functools.partial(jax.ShapeDtypeStruct, dtype=jnp.bfloat16)
    f32 = functools.partial(jax.ShapeDtypeStruct, dtype=jnp.float32)
    ids = expert_ids.reshape(tokens, 2).T
    gates = gate_probs.reshape(tokens, 2).T
    dout = d_out.reshape(tokens, width)
    part = w_out.shape[1]

    up, left, corner = pl.pallas_call(
        prepare,
        out_shape=(bf16((4 * tc, width)), bf16((4 * tr, width)), bf16((16, width))),
        in_specs=[ANY],
        out_specs=(VMEM,) * 3,
        scratch_shapes=[pltpu.VMEM((tr, tc, width), jnp.bfloat16), pltpu.SemaphoreType.DMA],
        compiler_params=pltpu.CompilerParams(vmem_limit_bytes=32 * 1024 * 1024),
        cost_estimate=pl.CostEstimate(flops=1 << 25, bytes_accessed=1 << 20, transcendentals=0),
    )(in_hbm(attn_win))
    up, left, corner, ids = lax.optimization_barrier((up, left, corner, ids))
    up, left, corner = edges(up, left, corner, 1)
    g_wire, masks, meta, x0, sel, w_own = pl.pallas_call(
        dispatch_g,
        out_shape=(
            bf16((n, WIDE)),
            bf16((3, n, tokens)),
            f32((tokens, tokens)),
            f32((tokens, width)),
            bf16((tokens, 4 * tc + 4 * tr + 16)),
            bf16((2, part, width)),
        ),
        in_specs=[ANY] * 8,
        out_specs=(VMEM,) * 6,
        scratch_shapes=[
            pltpu.SMEM((2,), jnp.int32),
            pltpu.VMEM((2, tokens), jnp.int32),
            pltpu.VMEM((2, tokens), jnp.float32),
        ]
        + [pltpu.VMEM((tr, tc, width), jnp.bfloat16)] * 3
        + [pltpu.SemaphoreType.DMA((8,))],
        compiler_params=pltpu.CompilerParams(vmem_limit_bytes=32 * 1024 * 1024),
        cost_estimate=pl.CostEstimate(
            flops=4 * 256 * n * WIDE, bytes_accessed=1 << 20, transcendentals=0
        ),
    )(
        *(
            in_hbm(v)
            for v in (
                shift_offsets, ids, gates, d_out, attn_win, shortcut,
                w_in.transpose(0, 2, 1), w_out,
            )
        )
    )
    n_x = lax.axis_size("dp") // 2
    near = [d for d in range(1, n_x) if d in (1, n_x - 1)]
    shards = dict(zip(near, relay([along_x(w_own, d) for d in near])))
    mine = [w_own] + [shards[d] if d in near else along_x(w_own, d) for d in range(1, n_x)]
    theirs = [other_core(v) for v in mine]
    sent, x = call(
        dispatch_u,
        (bf16((n, 2 * WIDE)), f32((tokens, width))),
        g_wire, masks, x0, sel, up, left, corner,
        flops=4 * 128 * n * WIDE, traffic=1 << 21,
    )
    returned, g_mine, g_theirs = experts(exchange(sent, n_ex), mine, theirs)
    swapped = other_core(g_theirs)
    returned = exchange(returned, n_ex)
    kept, *pieces = pair_sum(g_mine, swapped)
    arrived = [along_x(v, -d) for d, v in enumerate(pieces, 1)]
    ds, ds_keep, up_b, left_b, corner_b = call(
        functools.partial(combine_q, tr, tc),
        (
            bf16((tokens, width)),
            bf16((tokens, width)),
            bf16((4 * tc, width)),
            bf16((4 * tr, width)),
            bf16((16, width)),
        ),
        returned, meta, x, dout,
        flops=4 * tokens * n * WIDE, traffic=1 << 21,
    )
    down, right, corner_r = edges(up_b, left_b, corner_b, -1)
    block_out, d_gates, grad_in, grad_out = pl.pallas_call(
        combine_y,
        out_shape=(bf16((tokens, width)), f32((2, tokens)))
        + (pltpu.HBM((1, part, width), jnp.float32),) * 2,
        in_specs=[VMEM] * 4 + [ANY] + [VMEM] * (n_x - 1),
        out_specs=(VMEM, VMEM, ANY, ANY),
        scratch_shapes=[
            pltpu.VMEM(kept.shape, jnp.float32),
            pltpu.VMEM(kept.shape, jnp.float32),
            pltpu.SemaphoreType.DMA((3,)),
        ],
        compiler_params=pltpu.CompilerParams(vmem_limit_bytes=32 * 1024 * 1024),
        cost_estimate=pl.CostEstimate(
            flops=8 * tokens * n * WIDE, bytes_accessed=1 << 21, transcendentals=0
        ),
    )(returned, meta, x, dout, in_hbm(kept), *arrived)
    ds_keep, block_out = lax.optimization_barrier((ds_keep, block_out))
    d_attn = call(
        functools.partial(roll_back, tr, tc),
        bf16((tokens, width)),
        shift_offsets, ds_keep, down, right, corner_r,
        specs=[SMEM] + [VMEM] * 4,
        flops=2 * tokens * 256 * width, traffic=1 << 19,
    )
    tile = (tr, tc, width)
    return (
        block_out.reshape(tile),
        ds.reshape(tile),
        d_attn.reshape(tile),
        d_gates.T.reshape(1, 1, tokens, 2),
        grad_in.transpose(0, 2, 1),
        grad_out,
    )


def solution(mesh):
    tile = P("dp", "expert", None)
    pairs = P("dp", "expert", None, None)
    first, second = P("expert", None, "dp"), P("expert", "dp", None)
    return jax.shard_map(
        per_device,
        mesh=mesh,
        in_specs=(tile, tile, tile, pairs, pairs, P(), first, second),
        out_specs=(tile, tile, tile, pairs, first, second),
        check_vma=False,
    )
```

```python
import functools

import jax
import jax.numpy as jnp
from jax import lax
from jax.experimental import pallas as pl
from jax.experimental.pallas import tpu as pltpu
from jax.sharding import PartitionSpec as P

CAP = 5
WIRE_ROWS = 8
WIDE = 512
EPS = 1e-05
VMEM = pl.BlockSpec(memory_space=pltpu.VMEM)
ANY = pl.BlockSpec(memory_space=pl.ANY)
SMEM = pl.BlockSpec(memory_space=pltpu.SMEM)


def iota(shape, dim):
    return lax.broadcasted_iota(jnp.int32, shape, dim)


def ones_where(mask):
    return jnp.where(mask, 1.0, 0.0).astype(jnp.bfloat16)


def dot(a, b):
    return jnp.dot(a, b, preferred_element_type=jnp.float32)


def dot_t(a, b):
    return lax.dot_general(a, b, (((1,), (1,)), ((), ())), preferred_element_type=jnp.float32)


def t_dot(a, b):
    return lax.dot_general(a, b, (((0,), (0,)), ((), ())), preferred_element_type=jnp.float32)


def in_hbm(x):
    return pltpu.with_memory_space_constraint(x, pltpu.HBM)


def call(body, outs, *args, flops=0, traffic=0, specs=None, **kw):
    return pl.pallas_call(
        body,
        out_shape=outs,
        in_specs=[VMEM] * len(args) if specs is None else specs,
        out_specs=jax.tree.map(lambda _: VMEM, outs),
        compiler_params=pltpu.CompilerParams(vmem_limit_bytes=32 * 1024 * 1024),
        cost_estimate=pl.CostEstimate(flops=flops, bytes_accessed=traffic, transcendentals=0),
        **kw,
    )(*args)


def wire_masks(row, shape, dim):
    at = iota(shape, dim)
    pos = row & 7
    tail = row - pos + CAP + (pos >> 1)
    odd = (pos & 1) == 1
    left = jnp.where(odd, -1, tail)
    right = jnp.where(odd, tail, -1)
    return ones_where(at == row), ones_where(at == left), ones_where(at == right)


def from_wire(masks, wire):
    head, left, right = masks
    half = WIDE // 2
    return (
        dot(head, wire),
        dot(left, wire[:, :half]) + dot(right, wire[:, half:]),
    )


def to_wire(masks, rows, turned):
    head, left, right = masks
    f = t_dot if turned else dot
    tail = rows[:, WIDE:]
    return f(head, rows[:, :WIDE]) + jnp.concatenate([f(left, tail), f(right, tail)], axis=1)


def prepare(attn_hbm, up_ref, left_ref, corner_ref, attn_s, sem):
    copy = pltpu.make_async_copy(attn_hbm, attn_s, sem)
    copy.start()
    tr, tc, width = attn_s.shape
    tokens = tr * tc
    n = 4 * tr
    s = iota((n, 1), 0)
    edge = ones_where((s // 4) * tc + tc - 4 + s % 4 == iota((n, tokens), 1))
    copy.wait()
    attn = attn_s[...].reshape(tokens, width)
    up_ref[...] = attn[tokens - 4 * tc :]
    left = dot(edge, attn).astype(jnp.bfloat16)
    left_ref[...] = left
    corner_ref[...] = left[n - 16 :]


def dispatch_g(
    off_hbm, ids_hbm, gates_hbm, dout_hbm, attn_hbm, short_hbm, w1_hbm, w2_hbm,
    sent_ref, mask_ref, meta_ref, x_ref, sel_ref, w_ref,
    off_ref, ids_ref, gates_ref, dout_s, attn_s, short_s, sems,
):
    copies = [
        pltpu.make_async_copy(src, dst, sems.at[i])
        for i, (src, dst) in enumerate(
            (
                (off_hbm, off_ref),
                (ids_hbm, ids_ref),
                (gates_hbm, gates_ref),
                (attn_hbm, attn_s),
                (short_hbm, short_s),
                (dout_hbm, dout_s),
                (w1_hbm, w_ref.at[:, 0]),
                (w2_hbm, w_ref.at[:, 1]),
            )
        )
    ]
    for copy in copies:
        copy.start()
    for copy in copies[:6]:
        copy.wait()
    tr, tc, width = attn_s.shape
    tokens = tr * tc
    t = iota((tokens, 1), 0)
    inside, halo = places(t // tc - off_ref[0], t % tc - off_ref[1], tr, tc)
    sel_ref[...] = halo
    x_ref[...] = short_s[...].reshape(tokens, width).astype(jnp.float32) + dot(
        inside, attn_s[...].reshape(tokens, width)
    )
    n = sent_ref.shape[0]
    experts = n // WIRE_ROWS
    ids = ids_ref[...]
    rank = iota((experts, tokens), 0)
    first = jnp.where(ids[0:1] == rank, 1.0, 0.0)
    second = jnp.where(ids[1:2] == rank, 1.0, 0.0)
    earlier = ones_where(iota((tokens, tokens), 0) < iota((tokens, tokens), 1))
    before = dot((first + second).astype(jnp.bfloat16), earlier)
    row0 = ids[0:1] * WIRE_ROWS + jnp.sum(before * first, axis=0, keepdims=True).astype(jnp.int32)
    row1 = ids[1:2] * WIRE_ROWS + jnp.sum(before * second, axis=0, keepdims=True).astype(jnp.int32)
    at = iota((tokens, tokens), 0)
    table = jnp.where(at == 0, gates_ref[0:1], 0.0)
    table = jnp.where(at == 1, gates_ref[1:2], table)
    table = jnp.where(at == 2, row0.astype(jnp.float32), table)
    table = jnp.where(at == 3, row1.astype(jnp.float32), table)
    meta = table.T
    meta_ref[...] = meta
    dout = dout_s[...].reshape(tokens, width).astype(jnp.float32)
    sent = 0.0
    both = None
    for k, row in enumerate((row0, row1)):
        masks = wire_masks(row, (n, tokens), 0)
        sent = sent + to_wire(masks, (meta[:, k : k + 1] * dout).astype(jnp.bfloat16), False)
        both = masks if both is None else tuple(a + b for a, b in zip(both, masks))
    for m in range(3):
        mask_ref[m] = both[m]
    sent_ref[...] = sent.astype(jnp.bfloat16)
    for copy in copies[6:]:
        copy.wait()


def normalize(x):
    m = jnp.mean(x, axis=-1, keepdims=True)
    c = x - m
    r = lax.rsqrt(jnp.mean(c * c, axis=-1, keepdims=True) + EPS)
    return c * r, r


def places(i, j, tr, tc):
    tokens = i.shape[0]
    i_in = (i >= 0) & (i < tr)
    j_in = (j >= 0) & (j < tc)
    ei = jnp.where(i < 0, i + 4, i - tr)
    ej = jnp.where(j < 0, j + 4, j - tc)
    own = jnp.where(i_in & j_in, i * tc + j, -1)
    edge = jnp.where(
        i_in,
        jnp.where(j_in, -1, 4 * tc + i * 4 + ej),
        jnp.where(j_in, ei * tc + j, 4 * tc + 4 * tr + ei * 4 + ej),
    )
    count = 4 * tc + 4 * tr + 16
    return (
        ones_where(own == iota((tokens, tokens), 1)),
        ones_where(edge == iota((tokens, count), 1)),
    )


def dispatch_u(g_ref, mask_ref, x0_ref, sel_ref, up_ref, left_ref, corner_ref, sent_ref, x_ref):
    edge = jnp.concatenate([up_ref[...], left_ref[...], corner_ref[...]], axis=0)
    x = x0_ref[...] + dot(sel_ref[...], edge)
    x_ref[...] = x
    xhat, _ = normalize(x)
    masks = tuple(mask_ref[m] for m in range(3))
    sent_ref[:, :WIDE] = g_ref[...]
    sent_ref[:, WIDE:] = to_wire(masks, xhat.astype(jnp.bfloat16), False).astype(jnp.bfloat16)


def slot_masks(dim, peers):
    slots = peers * CAP
    s = iota((slots, 1) if dim else (1, slots), 1 - dim)
    row = (s % peers) * WIRE_ROWS + s // peers
    wire = peers * WIRE_ROWS
    return wire_masks(row, (slots, wire) if dim else (wire, slots), dim)


def send_slots(rows_of, out_ref, at):
    n = out_ref.shape[0]
    peers = min(32, n // WIRE_ROWS)
    rows, slots = peers * WIRE_ROWS, peers * CAP
    masks = slot_masks(0, peers)
    for b in range(n // rows):
        block = to_wire(masks, rows_of[b * slots : (b + 1) * slots], False)
        out_ref[b * rows : (b + 1) * rows, at : at + WIDE] = block.astype(jnp.bfloat16)


def experts_body(wire_ref, w_hbm, out_ref, grad_hbm, w_s, grad_s, u_s, g_s, in_sems, out_sems):
    parts, _, part, width = w_s.shape
    half = parts // 2
    hidden = half * part
    pieces = [(c, k) for c in range(2) for k in range(2)]
    ins = [
        pltpu.make_async_copy(
            w_hbm.at[pl.ds(c * half, half), k], w_s.at[pl.ds(c * half, half), k], in_sems.at[i]
        )
        for i, (c, k) in enumerate(pieces)
    ]
    outs = [
        pltpu.make_async_copy(
            grad_s.at[pl.ds(c * half, half), k], grad_hbm.at[pl.ds(c * half, half), k], out_sems.at[i]
        )
        for i, (c, k) in enumerate(pieces)
    ]
    for copy in ins:
        copy.start()
    n = wire_ref.shape[0]
    peers = min(32, n // WIRE_ROWS)
    rows, slots = peers * WIRE_ROWS, peers * CAP
    masks = slot_masks(1, peers)
    for b in range(n // rows):
        for at, dst in ((0, g_s), (WIDE, u_s)):
            head, tail = from_wire(masks, wire_ref[b * rows : (b + 1) * rows, at : at + WIDE])
            dst[b * slots : (b + 1) * slots, :WIDE] = head.astype(jnp.bfloat16)
            dst[b * slots : (b + 1) * slots, WIDE:] = tail.astype(jnp.bfloat16)
    u = u_s[...]
    g = g_s[...]

    def weights(c, k):
        return w_s[c * half : (c + 1) * half, k].reshape(hidden, width)

    pairs = []
    for c in range(2):
        ins[2 * c].wait()
        h = dot_t(u, weights(c, 0))
        ins[2 * c + 1].wait()
        pairs.append((h, dot_t(g, weights(c, 1))))
    acts = []
    for c, (h, da) in enumerate(pairs):
        cdf = 0.5 * (1.0 + lax.erf(h * 0.7071067811865476))
        pdf = jnp.exp(-0.5 * h * h) * 0.3989422804014327
        a = (h * cdf).astype(jnp.bfloat16)
        p = (da * (cdf + h * pdf)).astype(jnp.bfloat16)
        acts.append((p, a))
        for k, (left, right) in enumerate(((p, u), (a, g))):
            grad = t_dot(left, right).astype(jnp.bfloat16)
            grad_s[c * half : (c + 1) * half, k] = grad.reshape(half, part, width)
            outs[2 * c + k].start()
    q = dot(acts[0][0], weights(0, 0)) + dot(acts[1][0], weights(1, 0))
    y = dot(acts[0][1], weights(0, 1)) + dot(acts[1][1], weights(1, 1))
    send_slots(q.astype(jnp.bfloat16), out_ref, 0)
    send_slots(y.astype(jnp.bfloat16), out_ref, WIDE)
    for copy in outs:
        copy.wait()


def experts(wire, w):
    n = wire.shape[0]
    parts, _, part, width = w.shape
    slots = n // WIRE_ROWS * CAP
    hidden = parts * part
    return pl.pallas_call(
        experts_body,
        out_shape=(
            jax.ShapeDtypeStruct((n, 2 * WIDE), jnp.bfloat16),
            pltpu.HBM(w.shape, jnp.bfloat16),
        ),
        in_specs=[VMEM, ANY],
        out_specs=(VMEM, ANY),
        scratch_shapes=[
            pltpu.VMEM(w.shape, jnp.bfloat16),
            pltpu.VMEM(w.shape, jnp.bfloat16),
            pltpu.VMEM((slots, width), jnp.bfloat16),
            pltpu.VMEM((slots, width), jnp.bfloat16),
            pltpu.SemaphoreType.DMA((4,)),
            pltpu.SemaphoreType.DMA((4,)),
        ],
        compiler_params=pltpu.CompilerParams(vmem_limit_bytes=40 << 20),
        cost_estimate=pl.CostEstimate(
            flops=12 * slots * hidden * width,
            bytes_accessed=8 * hidden * width,
            transcendentals=2 * slots * hidden,
        ),
    )(wire, in_hbm(w))


def combine_q(tr, tc, wire_ref, meta_ref, x_ref, dout_ref, ds_ref, keep_ref, up_ref, left_ref, corner_ref):
    wire = wire_ref[:, :WIDE]
    tokens = x_ref.shape[0]
    both = None
    for k in range(2):
        row = meta_ref[:, 2 + k : 3 + k].astype(jnp.int32)
        masks = wire_masks(row, (tokens, wire.shape[0]), 1)
        both = masks if both is None else tuple(a + b for a, b in zip(both, masks))
    du = jnp.concatenate(from_wire(both, wire), axis=1)
    xhat, r = normalize(x_ref[...])
    dx = r * (
        du
        - jnp.mean(du, axis=-1, keepdims=True)
        - xhat * jnp.mean(du * xhat, axis=-1, keepdims=True)
    )
    ds = (dout_ref[...].astype(jnp.float32) + dx).astype(jnp.bfloat16)
    ds_ref[...] = ds
    keep_ref[...] = ds
    up_ref[...] = ds[: 4 * tc]
    n = 4 * tr
    s = iota((n, 1), 0)
    edge = dot(ones_where((s // 4) * tc + s % 4 == iota((n, tokens), 1)), ds).astype(jnp.bfloat16)
    left_ref[...] = edge
    corner_ref[...] = edge[:16]


def roll_back(tr, tc, off_ref, ds_ref, down_ref, right_ref, corner_ref, out_ref):
    t = iota((ds_ref.shape[0], 1), 0)
    inside, halo = places(t // tc + off_ref[0], t % tc + off_ref[1], tr, tc)
    edge = jnp.concatenate([down_ref[...], right_ref[...], corner_ref[...]], axis=0)
    out_ref[...] = (dot(inside, ds_ref[...]) + dot(halo, edge)).astype(jnp.bfloat16)


def combine_y(
    wire_ref, meta_ref, x_ref, dout_ref, grad_hbm, out_ref, dg_ref, first_hbm, second_hbm,
    grad_s, wide_s, sems,
):
    wides = (first_hbm, second_hbm)
    fetch = [pltpu.make_async_copy(grad_hbm.at[:, k], grad_s.at[:, k], sems.at[k]) for k in range(2)]
    store = [pltpu.make_async_copy(wide_s.at[:, k], wides[k], sems.at[2 + k]) for k in range(2)]
    for copy in fetch:
        copy.start()
    wire = wire_ref[:, WIDE:]
    dout = dout_ref[...].astype(jnp.float32)
    tokens = dout.shape[0]
    masks = [
        wire_masks(meta_ref[:, 2 + k : 3 + k].astype(jnp.int32), (tokens, wire.shape[0]), 1)
        for k in range(2)
    ]
    ys = [jnp.concatenate(from_wire(m, wire), axis=1) for m in masks]
    for k in range(2):
        fetch[k].wait()
        wide_s[:, k] = grad_s[:, k].astype(jnp.float32)
        store[k].start()
    total = x_ref[...]
    lane = iota((tokens, tokens), 1)
    table = jnp.zeros((tokens, tokens), jnp.float32)
    for k, y in enumerate(ys):
        total = total + meta_ref[:, k : k + 1] * y
        table = jnp.where(lane == k, jnp.sum(dout * y, axis=-1, keepdims=True), table)
    out_ref[...] = total.astype(jnp.bfloat16)
    dg_ref[...] = table.T[:2]
    for copy in store:
        copy.wait()


def exchange(wire, n):
    blocks = wire.reshape(n, WIRE_ROWS, wire.shape[-1])
    out = lax.all_to_all(blocks, "expert", split_axis=0, concat_axis=0, tiled=True)
    return out.reshape(wire.shape)


def edges(row_edge, col_edge, corner, step):
    n_dp, n_ex = lax.axis_size("dp"), lax.axis_size("expert")
    by_dp = [(i, (i + step) % n_dp) for i in range(n_dp)]
    by_ex = [(i, (i + step) % n_ex) for i in range(n_ex)]
    by_both = [
        (q * n_dp + p, (q + step) % n_ex * n_dp + (p + step) % n_dp)
        for q in range(n_ex)
        for p in range(n_dp)
    ]
    return (
        lax.ppermute(row_edge, "dp", by_dp),
        lax.ppermute(col_edge, "expert", by_ex),
        lax.ppermute(corner, ("expert", "dp"), by_both),
    )


def per_device(attn_win, shortcut, d_out, expert_ids, gate_probs, shift_offsets, w_in, w_out):
    tr, tc, width = attn_win.shape
    tokens = tr * tc
    n_ex = lax.axis_size("expert")
    n = n_ex * WIRE_ROWS
    bf16 = functools.partial(jax.ShapeDtypeStruct, dtype=jnp.bfloat16)
    f32 = functools.partial(jax.ShapeDtypeStruct, dtype=jnp.float32)
    ids = expert_ids.reshape(tokens, 2).T
    gates = gate_probs.reshape(tokens, 2).T
    dout = d_out.reshape(tokens, width)
    part = w_out.shape[1]

    up, left, corner = pl.pallas_call(
        prepare,
        out_shape=(bf16((4 * tc, width)), bf16((4 * tr, width)), bf16((16, width))),
        in_specs=[ANY],
        out_specs=(VMEM,) * 3,
        scratch_shapes=[pltpu.VMEM((tr, tc, width), jnp.bfloat16), pltpu.SemaphoreType.DMA],
        compiler_params=pltpu.CompilerParams(vmem_limit_bytes=32 * 1024 * 1024),
        cost_estimate=pl.CostEstimate(flops=1 << 25, bytes_accessed=1 << 20, transcendentals=0),
    )(in_hbm(attn_win))
    up, left, corner = edges(up, left, corner, 1)
    g_wire, masks, meta, x0, sel, w_own = pl.pallas_call(
        dispatch_g,
        out_shape=(
            bf16((n, WIDE)),
            bf16((3, n, tokens)),
            f32((tokens, tokens)),
            f32((tokens, width)),
            bf16((tokens, 4 * tc + 4 * tr + 16)),
            bf16((1, 2, part, width)),
        ),
        in_specs=[ANY] * 8,
        out_specs=(VMEM,) * 6,
        scratch_shapes=[
            pltpu.SMEM((2,), jnp.int32),
            pltpu.VMEM((2, tokens), jnp.int32),
            pltpu.VMEM((2, tokens), jnp.float32),
        ]
        + [pltpu.VMEM((tr, tc, width), jnp.bfloat16)] * 3
        + [pltpu.SemaphoreType.DMA((8,))],
        compiler_params=pltpu.CompilerParams(vmem_limit_bytes=32 * 1024 * 1024),
        cost_estimate=pl.CostEstimate(
            flops=1 << 36, bytes_accessed=1 << 20, transcendentals=0
        ),
    )(
        *(
            in_hbm(v)
            for v in (
                shift_offsets, ids, gates, d_out, attn_win, shortcut,
                w_in.transpose(0, 2, 1), w_out,
            )
        )
    )
    w_all = lax.all_gather(w_own, "dp", axis=0, tiled=True)
    sent, x = call(
        dispatch_u,
        (bf16((n, 2 * WIDE)), f32((tokens, width))),
        g_wire, masks, x0, sel, up, left, corner,
        flops=1 << 36, traffic=1 << 21,
    )
    returned, grads = experts(exchange(sent, n_ex), w_all)
    returned = exchange(returned, n_ex)
    grad = lax.psum_scatter(grads, "dp", scatter_dimension=0, tiled=True)
    ds, ds_keep, up_b, left_b, corner_b = call(
        functools.partial(combine_q, tr, tc),
        (
            bf16((tokens, width)),
            bf16((tokens, width)),
            bf16((4 * tc, width)),
            bf16((4 * tr, width)),
            bf16((16, width)),
        ),
        returned, meta, x, dout,
        flops=4 * tokens * n * WIDE, traffic=1 << 21,
    )
    down, right, corner_r = edges(up_b, left_b, corner_b, -1)
    block_out, d_gates, grad_in, grad_out = pl.pallas_call(
        combine_y,
        out_shape=(bf16((tokens, width)), f32((2, tokens)))
        + (pltpu.HBM((1, part, width), jnp.float32),) * 2,
        in_specs=[VMEM] * 4 + [ANY],
        out_specs=(VMEM, VMEM, ANY, ANY),
        scratch_shapes=[
            pltpu.VMEM(grad.shape, jnp.bfloat16),
            pltpu.VMEM(grad.shape, jnp.float32),
            pltpu.SemaphoreType.DMA((4,)),
        ],
        compiler_params=pltpu.CompilerParams(vmem_limit_bytes=32 * 1024 * 1024),
        cost_estimate=pl.CostEstimate(
            flops=8 * tokens * n * WIDE, bytes_accessed=1 << 21, transcendentals=0
        ),
    )(returned, meta, x, dout, in_hbm(grad))
    ds_keep, block_out = lax.optimization_barrier((ds_keep, block_out))
    d_attn = call(
        functools.partial(roll_back, tr, tc),
        bf16((tokens, width)),
        shift_offsets, ds_keep, down, right, corner_r,
        specs=[SMEM] + [VMEM] * 4,
        flops=2 * tokens * 256 * width, traffic=1 << 19,
    )
    tile = (tr, tc, width)
    return (
        block_out.reshape(tile),
        ds.reshape(tile),
        d_attn.reshape(tile),
        d_gates.T.reshape(1, 1, tokens, 2),
        grad_in.transpose(0, 2, 1),
        grad_out,
    )


def solution(mesh):
    tile = P("dp", "expert", None)
    pairs = P("dp", "expert", None, None)
    first, second = P("expert", None, "dp"), P("expert", "dp", None)
    return jax.shard_map(
        per_device,
        mesh=mesh,
        in_specs=(tile, tile, tile, pairs, pairs, P(), first, second),
        out_specs=(tile, tile, tile, pairs, first, second),
        check_vma=False,
    )
```

```python
import functools

import jax
import jax.numpy as jnp
from jax import lax
from jax.experimental import pallas as pl
from jax.experimental.pallas import tpu as pltpu
from jax.sharding import PartitionSpec as P

CAP = 5
WIRE_ROWS = 8
WIDE = 512
EPS = 1e-05
VMEM = pl.BlockSpec(memory_space=pltpu.VMEM)
ANY = pl.BlockSpec(memory_space=pl.ANY)
SMEM = pl.BlockSpec(memory_space=pltpu.SMEM)


def iota(shape, dim):
    return lax.broadcasted_iota(jnp.int32, shape, dim)


def ones_where(mask):
    return jnp.where(mask, 1.0, 0.0).astype(jnp.bfloat16)


def dot(a, b):
    return jnp.dot(a, b, preferred_element_type=jnp.float32)


def dot_t(a, b):
    return lax.dot_general(a, b, (((1,), (1,)), ((), ())), preferred_element_type=jnp.float32)


def t_dot(a, b):
    return lax.dot_general(a, b, (((0,), (0,)), ((), ())), preferred_element_type=jnp.float32)


def in_hbm(x):
    return pltpu.with_memory_space_constraint(x, pltpu.HBM)


def call(body, outs, *args, flops=0, traffic=0, specs=None, **kw):
    return pl.pallas_call(
        body,
        out_shape=outs,
        in_specs=[VMEM] * len(args) if specs is None else specs,
        out_specs=jax.tree.map(lambda _: VMEM, outs),
        compiler_params=pltpu.CompilerParams(vmem_limit_bytes=32 * 1024 * 1024),
        cost_estimate=pl.CostEstimate(flops=flops, bytes_accessed=traffic, transcendentals=0),
        **kw,
    )(*args)


def wire_masks(row, shape, dim):
    at = iota(shape, dim)
    pos = row & 7
    tail = row - pos + CAP + (pos >> 1)
    odd = (pos & 1) == 1
    left = jnp.where(odd, -1, tail)
    right = jnp.where(odd, tail, -1)
    return ones_where(at == row), ones_where(at == left), ones_where(at == right)


def from_wire(masks, wire):
    head, left, right = masks
    half = WIDE // 2
    return (
        dot(head, wire),
        dot(left, wire[:, :half]) + dot(right, wire[:, half:]),
    )


def to_wire(masks, rows, turned):
    head, left, right = masks
    f = t_dot if turned else dot
    tail = rows[:, WIDE:]
    return f(head, rows[:, :WIDE]) + jnp.concatenate([f(left, tail), f(right, tail)], axis=1)


def prepare(attn_hbm, up_ref, left_ref, corner_ref, attn_s, sem):
    copy = pltpu.make_async_copy(attn_hbm, attn_s, sem)
    copy.start()
    tr, tc, width = attn_s.shape
    tokens = tr * tc
    n = 4 * tr
    s = iota((n, 1), 0)
    edge = ones_where((s // 4) * tc + tc - 4 + s % 4 == iota((n, tokens), 1))
    copy.wait()
    attn = attn_s[...].reshape(tokens, width)
    up_ref[...] = attn[tokens - 4 * tc :]
    left = dot(edge, attn).astype(jnp.bfloat16)
    left_ref[...] = left
    corner_ref[...] = left[n - 16 :]


def join_body(w1_hbm, w2_hbm, w_ref, sems):
    copies = [
        pltpu.make_async_copy(src, w_ref.at[:, k], sems.at[k])
        for k, src in enumerate((w1_hbm, w2_hbm))
    ]
    for copy in copies:
        copy.start()
    for copy in copies:
        copy.wait()


def join(w1, w2):
    return pl.pallas_call(
        join_body,
        out_shape=jax.ShapeDtypeStruct((1, 2, *w2.shape[1:]), w2.dtype),
        in_specs=[ANY] * 2,
        out_specs=VMEM,
        scratch_shapes=[pltpu.SemaphoreType.DMA((2,))],
        compiler_params=pltpu.CompilerParams(vmem_limit_bytes=32 * 1024 * 1024),
        cost_estimate=pl.CostEstimate(flops=0, bytes_accessed=8 * w2.size, transcendentals=0),
    )(in_hbm(w1), in_hbm(w2))


def dispatch_g(
    off_hbm, ids_hbm, gates_hbm, dout_hbm, attn_hbm, short_hbm,
    sent_ref, mask_ref, meta_ref, x_ref, sel_ref,
    off_ref, ids_ref, gates_ref, dout_s, attn_s, short_s, sems,
):
    copies = [
        pltpu.make_async_copy(src, dst, sems.at[i])
        for i, (src, dst) in enumerate(
            (
                (off_hbm, off_ref),
                (ids_hbm, ids_ref),
                (gates_hbm, gates_ref),
                (attn_hbm, attn_s),
                (short_hbm, short_s),
                (dout_hbm, dout_s),
            )
        )
    ]
    for copy in copies:
        copy.start()
    for copy in copies:
        copy.wait()
    tr, tc, width = attn_s.shape
    tokens = tr * tc
    t = iota((tokens, 1), 0)
    inside, halo = places(t // tc - off_ref[0], t % tc - off_ref[1], tr, tc)
    sel_ref[...] = halo
    x_ref[...] = short_s[...].reshape(tokens, width).astype(jnp.float32) + dot(
        inside, attn_s[...].reshape(tokens, width)
    )
    n = sent_ref.shape[0]
    experts = n // WIRE_ROWS
    ids = ids_ref[...]
    rank = iota((experts, tokens), 0)
    first = jnp.where(ids[0:1] == rank, 1.0, 0.0)
    second = jnp.where(ids[1:2] == rank, 1.0, 0.0)
    earlier = ones_where(iota((tokens, tokens), 0) < iota((tokens, tokens), 1))
    before = dot((first + second).astype(jnp.bfloat16), earlier)
    row0 = ids[0:1] * WIRE_ROWS + jnp.sum(before * first, axis=0, keepdims=True).astype(jnp.int32)
    row1 = ids[1:2] * WIRE_ROWS + jnp.sum(before * second, axis=0, keepdims=True).astype(jnp.int32)
    at = iota((tokens, tokens), 0)
    table = jnp.where(at == 0, gates_ref[0:1], 0.0)
    table = jnp.where(at == 1, gates_ref[1:2], table)
    table = jnp.where(at == 2, row0.astype(jnp.float32), table)
    table = jnp.where(at == 3, row1.astype(jnp.float32), table)
    meta = table.T
    meta_ref[...] = meta
    dout = dout_s[...].reshape(tokens, width).astype(jnp.float32)
    sent = 0.0
    both = None
    for k, row in enumerate((row0, row1)):
        masks = wire_masks(row, (n, tokens), 0)
        sent = sent + to_wire(masks, (meta[:, k : k + 1] * dout).astype(jnp.bfloat16), False)
        both = masks if both is None else tuple(a + b for a, b in zip(both, masks))
    for m in range(3):
        mask_ref[m] = both[m]
    sent_ref[...] = sent.astype(jnp.bfloat16)


def normalize(x):
    m = jnp.mean(x, axis=-1, keepdims=True)
    c = x - m
    r = lax.rsqrt(jnp.mean(c * c, axis=-1, keepdims=True) + EPS)
    return c * r, r


def places(i, j, tr, tc):
    tokens = i.shape[0]
    i_in = (i >= 0) & (i < tr)
    j_in = (j >= 0) & (j < tc)
    ei = jnp.where(i < 0, i + 4, i - tr)
    ej = jnp.where(j < 0, j + 4, j - tc)
    own = jnp.where(i_in & j_in, i * tc + j, -1)
    edge = jnp.where(
        i_in,
        jnp.where(j_in, -1, 4 * tc + i * 4 + ej),
        jnp.where(j_in, ei * tc + j, 4 * tc + 4 * tr + ei * 4 + ej),
    )
    count = 4 * tc + 4 * tr + 16
    return (
        ones_where(own == iota((tokens, tokens), 1)),
        ones_where(edge == iota((tokens, count), 1)),
    )


def dispatch_u(g_ref, mask_ref, x0_ref, sel_ref, up_ref, left_ref, corner_ref, sent_ref, x_ref):
    edge = jnp.concatenate([up_ref[...], left_ref[...], corner_ref[...]], axis=0)
    x = x0_ref[...] + dot(sel_ref[...], edge)
    x_ref[...] = x
    xhat, _ = normalize(x)
    masks = tuple(mask_ref[m] for m in range(3))
    sent_ref[:, :WIDE] = g_ref[...]
    sent_ref[:, WIDE:] = to_wire(masks, xhat.astype(jnp.bfloat16), False).astype(jnp.bfloat16)


def slot_masks(dim, peers):
    slots = peers * CAP
    s = iota((slots, 1) if dim else (1, slots), 1 - dim)
    row = (s % peers) * WIRE_ROWS + s // peers
    wire = peers * WIRE_ROWS
    return wire_masks(row, (slots, wire) if dim else (wire, slots), dim)


def send_slots(rows_of, out_ref, at):
    n = out_ref.shape[0]
    peers = min(32, n // WIRE_ROWS)
    rows, slots = peers * WIRE_ROWS, peers * CAP
    masks = slot_masks(0, peers)
    for b in range(n // rows):
        block = to_wire(masks, rows_of[b * slots : (b + 1) * slots], False)
        out_ref[b * rows : (b + 1) * rows, at : at + WIDE] = block.astype(jnp.bfloat16)


def experts_body(wire_ref, w_hbm, out_ref, grad_hbm, w_s, grad_s, u_s, g_s, in_sems, out_sems):
    parts, _, part, width = w_s.shape
    half = parts // 2
    hidden = half * part
    pieces = [(c, k) for c in range(2) for k in range(2)]
    ins = [
        pltpu.make_async_copy(
            w_hbm.at[pl.ds(c * half, half), k], w_s.at[pl.ds(c * half, half), k], in_sems.at[i]
        )
        for i, (c, k) in enumerate(pieces)
    ]
    outs = [
        pltpu.make_async_copy(
            grad_s.at[pl.ds(c * half, half), k], grad_hbm.at[pl.ds(c * half, half), k], out_sems.at[i]
        )
        for i, (c, k) in enumerate(pieces)
    ]
    for copy in ins:
        copy.start()
    n = wire_ref.shape[0]
    peers = min(32, n // WIRE_ROWS)
    rows, slots = peers * WIRE_ROWS, peers * CAP
    masks = slot_masks(1, peers)
    for b in range(n // rows):
        for at, dst in ((0, g_s), (WIDE, u_s)):
            head, tail = from_wire(masks, wire_ref[b * rows : (b + 1) * rows, at : at + WIDE])
            dst[b * slots : (b + 1) * slots, :WIDE] = head.astype(jnp.bfloat16)
            dst[b * slots : (b + 1) * slots, WIDE:] = tail.astype(jnp.bfloat16)
    u = u_s[...]
    g = g_s[...]

    def weights(c, k):
        return w_s[c * half : (c + 1) * half, k].reshape(hidden, width)

    pairs = []
    for c in range(2):
        ins[2 * c].wait()
        h = dot_t(u, weights(c, 0))
        ins[2 * c + 1].wait()
        pairs.append((h, dot_t(g, weights(c, 1))))
    acts = []
    for c, (h, da) in enumerate(pairs):
        cdf = 0.5 * (1.0 + lax.erf(h * 0.7071067811865476))
        pdf = jnp.exp(-0.5 * h * h) * 0.3989422804014327
        a = (h * cdf).astype(jnp.bfloat16)
        p = (da * (cdf + h * pdf)).astype(jnp.bfloat16)
        acts.append((p, a))
        for k, (left, right) in enumerate(((p, u), (a, g))):
            grad = t_dot(left, right).astype(jnp.bfloat16)
            grad_s[c * half : (c + 1) * half, k] = grad.reshape(half, part, width)
            outs[2 * c + k].start()
    q = dot(acts[0][0], weights(0, 0)) + dot(acts[1][0], weights(1, 0))
    y = dot(acts[0][1], weights(0, 1)) + dot(acts[1][1], weights(1, 1))
    send_slots(q.astype(jnp.bfloat16), out_ref, 0)
    send_slots(y.astype(jnp.bfloat16), out_ref, WIDE)
    for copy in outs:
        copy.wait()


def experts(wire, w):
    n = wire.shape[0]
    parts, _, part, width = w.shape
    slots = n // WIRE_ROWS * CAP
    hidden = parts * part
    return pl.pallas_call(
        experts_body,
        out_shape=(
            jax.ShapeDtypeStruct((n, 2 * WIDE), jnp.bfloat16),
            pltpu.HBM(w.shape, jnp.bfloat16),
        ),
        in_specs=[VMEM, ANY],
        out_specs=(VMEM, ANY),
        scratch_shapes=[
            pltpu.VMEM(w.shape, jnp.bfloat16),
            pltpu.VMEM(w.shape, jnp.bfloat16),
            pltpu.VMEM((slots, width), jnp.bfloat16),
            pltpu.VMEM((slots, width), jnp.bfloat16),
            pltpu.SemaphoreType.DMA((4,)),
            pltpu.SemaphoreType.DMA((4,)),
        ],
        compiler_params=pltpu.CompilerParams(vmem_limit_bytes=40 << 20),
        cost_estimate=pl.CostEstimate(
            flops=12 * slots * hidden * width,
            bytes_accessed=8 * hidden * width,
            transcendentals=2 * slots * hidden,
        ),
    )(wire, in_hbm(w))


def combine_q(tr, tc, wire_ref, meta_ref, x_ref, dout_ref, ds_ref, keep_ref, up_ref, left_ref, corner_ref):
    wire = wire_ref[:, :WIDE]
    tokens = x_ref.shape[0]
    both = None
    for k in range(2):
        row = meta_ref[:, 2 + k : 3 + k].astype(jnp.int32)
        masks = wire_masks(row, (tokens, wire.shape[0]), 1)
        both = masks if both is None else tuple(a + b for a, b in zip(both, masks))
    du = jnp.concatenate(from_wire(both, wire), axis=1)
    xhat, r = normalize(x_ref[...])
    dx = r * (
        du
        - jnp.mean(du, axis=-1, keepdims=True)
        - xhat * jnp.mean(du * xhat, axis=-1, keepdims=True)
    )
    ds = (dout_ref[...].astype(jnp.float32) + dx).astype(jnp.bfloat16)
    ds_ref[...] = ds
    keep_ref[...] = ds
    up_ref[...] = ds[: 4 * tc]
    n = 4 * tr
    s = iota((n, 1), 0)
    edge = dot(ones_where((s // 4) * tc + s % 4 == iota((n, tokens), 1)), ds).astype(jnp.bfloat16)
    left_ref[...] = edge
    corner_ref[...] = edge[:16]


def roll_back(tr, tc, off_ref, ds_ref, down_ref, right_ref, corner_ref, out_ref):
    t = iota((ds_ref.shape[0], 1), 0)
    inside, halo = places(t // tc + off_ref[0], t % tc + off_ref[1], tr, tc)
    edge = jnp.concatenate([down_ref[...], right_ref[...], corner_ref[...]], axis=0)
    out_ref[...] = (dot(inside, ds_ref[...]) + dot(halo, edge)).astype(jnp.bfloat16)


def combine_y(
    wire_ref, meta_ref, x_ref, dout_ref, grad_hbm, out_ref, dg_ref, first_hbm, second_hbm,
    grad_s, wide_s, sems,
):
    wides = (first_hbm, second_hbm)
    fetch = [pltpu.make_async_copy(grad_hbm.at[:, k], grad_s.at[:, k], sems.at[k]) for k in range(2)]
    store = [pltpu.make_async_copy(wide_s.at[:, k], wides[k], sems.at[2 + k]) for k in range(2)]
    for copy in fetch:
        copy.start()
    wire = wire_ref[:, WIDE:]
    dout = dout_ref[...].astype(jnp.float32)
    tokens = dout.shape[0]
    masks = [
        wire_masks(meta_ref[:, 2 + k : 3 + k].astype(jnp.int32), (tokens, wire.shape[0]), 1)
        for k in range(2)
    ]
    ys = [jnp.concatenate(from_wire(m, wire), axis=1) for m in masks]
    for k in range(2):
        fetch[k].wait()
        wide_s[:, k] = grad_s[:, k].astype(jnp.float32)
        store[k].start()
    total = x_ref[...]
    lane = iota((tokens, tokens), 1)
    table = jnp.zeros((tokens, tokens), jnp.float32)
    for k, y in enumerate(ys):
        total = total + meta_ref[:, k : k + 1] * y
        table = jnp.where(lane == k, jnp.sum(dout * y, axis=-1, keepdims=True), table)
    out_ref[...] = total.astype(jnp.bfloat16)
    dg_ref[...] = table.T[:2]
    for copy in store:
        copy.wait()


def exchange(wire, n):
    blocks = wire.reshape(n, WIRE_ROWS, wire.shape[-1])
    out = lax.all_to_all(blocks, "expert", split_axis=0, concat_axis=0, tiled=True)
    return out.reshape(wire.shape)


def edges(row_edge, col_edge, corner, step):
    n_dp, n_ex = lax.axis_size("dp"), lax.axis_size("expert")
    by_dp = [(i, (i + step) % n_dp) for i in range(n_dp)]
    by_ex = [(i, (i + step) % n_ex) for i in range(n_ex)]
    by_both = [
        (q * n_dp + p, (q + step) % n_ex * n_dp + (p + step) % n_dp)
        for q in range(n_ex)
        for p in range(n_dp)
    ]
    row_edge = lax.ppermute(row_edge, "dp", by_dp)
    corner = lax.ppermute(corner, ("expert", "dp"), by_both)
    col_edge = lax.ppermute(col_edge, "expert", by_ex)
    return row_edge, col_edge, corner


def per_device(attn_win, shortcut, d_out, expert_ids, gate_probs, shift_offsets, w_in, w_out):
    tr, tc, width = attn_win.shape
    tokens = tr * tc
    n_ex = lax.axis_size("expert")
    n = n_ex * WIRE_ROWS
    bf16 = functools.partial(jax.ShapeDtypeStruct, dtype=jnp.bfloat16)
    f32 = functools.partial(jax.ShapeDtypeStruct, dtype=jnp.float32)
    ids = expert_ids.reshape(tokens, 2).T
    gates = gate_probs.reshape(tokens, 2).T
    dout = d_out.reshape(tokens, width)
    part = w_out.shape[1]

    up, left, corner = pl.pallas_call(
        prepare,
        out_shape=(bf16((4 * tc, width)), bf16((4 * tr, width)), bf16((16, width))),
        in_specs=[ANY],
        out_specs=(VMEM,) * 3,
        scratch_shapes=[pltpu.VMEM((tr, tc, width), jnp.bfloat16), pltpu.SemaphoreType.DMA],
        compiler_params=pltpu.CompilerParams(vmem_limit_bytes=32 * 1024 * 1024),
        cost_estimate=pl.CostEstimate(flops=1 << 25, bytes_accessed=1 << 20, transcendentals=0),
    )(in_hbm(attn_win))
    w_in, left = lax.optimization_barrier((w_in, left))
    w_own = join(w_in.transpose(0, 2, 1), w_out)
    w_all = lax.all_gather(w_own, "dp", axis=0, tiled=True)
    up, left, corner = edges(up, left, corner, 1)
    g_wire, masks, meta, x0, sel = pl.pallas_call(
        dispatch_g,
        out_shape=(
            bf16((n, WIDE)),
            bf16((3, n, tokens)),
            f32((tokens, tokens)),
            f32((tokens, width)),
            bf16((tokens, 4 * tc + 4 * tr + 16)),
        ),
        in_specs=[ANY] * 6,
        out_specs=(VMEM,) * 5,
        scratch_shapes=[
            pltpu.SMEM((2,), jnp.int32),
            pltpu.VMEM((2, tokens), jnp.int32),
            pltpu.VMEM((2, tokens), jnp.float32),
        ]
        + [pltpu.VMEM((tr, tc, width), jnp.bfloat16)] * 3
        + [pltpu.SemaphoreType.DMA((6,))],
        compiler_params=pltpu.CompilerParams(vmem_limit_bytes=32 * 1024 * 1024),
        cost_estimate=pl.CostEstimate(
            flops=1 << 36, bytes_accessed=1 << 20, transcendentals=0
        ),
    )(*(in_hbm(v) for v in (shift_offsets, ids, gates, d_out, attn_win, shortcut)))
    sent, x = call(
        dispatch_u,
        (bf16((n, 2 * WIDE)), f32((tokens, width))),
        g_wire, masks, x0, sel, up, left, corner,
        flops=4 * 128 * n * WIDE, traffic=1 << 21,
    )
    returned, grads = experts(exchange(sent, n_ex), w_all)
    returned = exchange(returned, n_ex)
    grad = lax.psum_scatter(grads, "dp", scatter_dimension=0, tiled=True)
    ds, ds_keep, up_b, left_b, corner_b = call(
        functools.partial(combine_q, tr, tc),
        (
            bf16((tokens, width)),
            bf16((tokens, width)),
            bf16((4 * tc, width)),
            bf16((4 * tr, width)),
            bf16((16, width)),
        ),
        returned, meta, x, dout,
        flops=4 * tokens * n * WIDE, traffic=1 << 21,
    )
    down, right, corner_r = edges(up_b, left_b, corner_b, -1)
    block_out, d_gates, grad_in, grad_out = pl.pallas_call(
        combine_y,
        out_shape=(bf16((tokens, width)), f32((2, tokens)))
        + (pltpu.HBM((1, part, width), jnp.float32),) * 2,
        in_specs=[VMEM] * 4 + [ANY],
        out_specs=(VMEM, VMEM, ANY, ANY),
        scratch_shapes=[
            pltpu.VMEM(grad.shape, jnp.bfloat16),
            pltpu.VMEM(grad.shape, jnp.float32),
            pltpu.SemaphoreType.DMA((4,)),
        ],
        compiler_params=pltpu.CompilerParams(vmem_limit_bytes=32 * 1024 * 1024),
        cost_estimate=pl.CostEstimate(
            flops=8 * tokens * n * WIDE, bytes_accessed=1 << 21, transcendentals=0
        ),
    )(returned, meta, x, dout, in_hbm(grad))
    ds_keep, block_out = lax.optimization_barrier((ds_keep, block_out))
    d_attn = call(
        functools.partial(roll_back, tr, tc),
        bf16((tokens, width)),
        shift_offsets, ds_keep, down, right, corner_r,
        specs=[SMEM] + [VMEM] * 4,
        flops=2 * tokens * 256 * width, traffic=1 << 19,
    )
    tile = (tr, tc, width)
    return (
        block_out.reshape(tile),
        ds.reshape(tile),
        d_attn.reshape(tile),
        d_gates.T.reshape(1, 1, tokens, 2),
        grad_in.transpose(0, 2, 1),
        grad_out,
    )


def solution(mesh):
    tile = P("dp", "expert", None)
    pairs = P("dp", "expert", None, None)
    first, second = P("expert", None, "dp"), P("expert", "dp", None)
    return jax.shard_map(
        per_device,
        mesh=mesh,
        in_specs=(tile, tile, tile, pairs, pairs, P(), first, second),
        out_specs=(tile, tile, tile, pairs, first, second),
        check_vma=False,
    )
```
